256 devices in a mesh: gx: 8 (over z), gy: 4 (over y), gz: 8 (over x, core).
Axes of the slice: x: 4, y: 4, z: 8, core: 2. Of those that a mesh axis runs over, the one named last changes fastest.
Arguments:
- adjoint_rhs: float32 [8, 4, 8, 8, 1024], P('gx', 'gy', 'gz'), may hold values from -120 to 120
- dual_operator: float32 [8, 4, 8, 1024, 1024], P('gx', 'gy', 'gz'), may hold values from -0.5 to 1.5, as said below
- dirichlet: float32 [8, 4, 8, 1024, 1024], P('gx', 'gy', 'gz'), may hold values from -0.5 to 2.5, as said below
- geneo_modes: float32 [8, 4, 8, 32, 1024], P('gx', 'gy', 'gz'), may hold values from -0.1875 to 0.1875
- coarse_inverse: float32 [8, 4, 8, 32, 8192], P('gx', 'gy', 'gz'), may hold values from -0.5 to 1.5, as said below
- partner_slot: int32 [8, 4, 8, 1024], P('gx', 'gy', 'gz'), may hold values from 0 to 1023, as said below
- jump_sign: int32 [8, 4, 8, 1024], P('gx', 'gy', 'gz'), may hold values from -1 to 1, as said below
- mode_count: int32 [8, 4, 8], P('gx', 'gy', 'gz'), may hold values from 8 to 32
Outputs:
- dual_solution: float32 [8, 4, 8, 8, 1024], P('gx', 'gy', 'gz')
- interface_force: float32 [8, 4, 8, 8, 1024], P('gx', 'gy', 'gz')
The draws below stay inside these ranges and needn't reach their ends.
Inputs may be any that keep to these rules, and one draw needn't show every extreme that they name: `dual_operator`: symmetric positive definite. `dirichlet`: symmetric positive definite. `coarse_inverse`: the whole 8192-order coarse inverse, rows and columns ordered as the coefficients, is symmetric positive definite. `partner_slot`: for a paired slot of block d, the partner slot lies in the neighbour's block of direction -d, and the neighbour's partner of it is this slot again. On unpaired slots the value is the slot's own index. `jump_sign`: A paired slot and its partner have opposite signs.
All inputs are finite; a program needn't handle non-finite values.
Results may differ from the reference program's by a relative error of at most 0.0003.
Values sent between devices are 32-bit elements; how exact they have to be, the bound alone decides.
A program may use at most 64 MiB of HBM per device.

```python
import jax
import jax.numpy as jnp
from jax import lax

DUAL_SIZE = 1024
FACE_SLOTS = 144
EDGE_SLOTS = 12
CORNER_SLOTS = 2
GENEO_MODES = 32
ADJOINT_LOADS = 8
DUAL_STEPS = 3
ACROSS_FIRST = 8
ACROSS_SECOND = 4
ACROSS_THIRD = 8
COARSE_SIZE = 8192


def block_list_drawn():
    blocks = []
    cursor = 0
    for shift_first in (-1, 0, 1):
        for shift_second in (-1, 0, 1):
            for shift_third in (-1, 0, 1):
                nonzero = abs(shift_first) + abs(shift_second) + abs(shift_third)
                if nonzero == 0:
                    continue
                extent = FACE_SLOTS if nonzero == 1 else EDGE_SLOTS if nonzero == 2 else CORNER_SLOTS
                blocks.append(((shift_first, shift_second, shift_third), cursor, extent))
                cursor += extent
    return blocks


def spd_block(block_key, order_size, lowest, highest):
    diag_key, noise_key = jax.random.split(block_key)
    diagonal = jnp.exp(jax.random.uniform(diag_key, (order_size,), jnp.float32, jnp.log(lowest), jnp.log(highest)))
    noise = jax.random.normal(noise_key, (order_size, order_size), jnp.float32)
    symmetric = (noise + noise.T) * (0.25 / jnp.sqrt(2.0 * order_size))
    off_diagonal = 1.0 - jnp.eye(order_size, dtype=jnp.float32)
    return symmetric * off_diagonal + jnp.diag(diagonal)


def draw_adjoint_rhs(key, part):
    device_total = ACROSS_FIRST * ACROSS_SECOND * ACROSS_THIRD
    shape = (device_total, ADJOINT_LOADS, DUAL_SIZE)
    parts_keys = jax.random.split(jax.random.fold_in(key, 17), 3)
    position = jnp.arange(device_total, dtype=jnp.float32) / (device_total - 1)
    device_scale = (3.0 ** position)[:, None, None]
    slot_scale = jnp.exp(jax.random.uniform(parts_keys[0], (device_total, 1, DUAL_SIZE), jnp.float32, jnp.log(0.3), jnp.log(3.0)))
    load_scale = jnp.exp(jax.random.uniform(parts_keys[1], (1, ADJOINT_LOADS, 1), jnp.float32, jnp.log(0.5), jnp.log(2.0)))
    base = jnp.clip(jax.random.normal(parts_keys[2], shape, jnp.float32), -4.0, 4.0)
    values = base * device_scale * slot_scale * load_scale
    return values.reshape(ACROSS_FIRST, ACROSS_SECOND, ACROSS_THIRD, ADJOINT_LOADS, DUAL_SIZE)


def operator_blocks(key, lowest, highest):
    device_total = ACROSS_FIRST * ACROSS_SECOND * ACROSS_THIRD
    device_keys = jax.random.split(key, device_total)

    def make_block(one_key):
        return spd_block(one_key, DUAL_SIZE, lowest, highest)
    blocks = lax.map(make_block, device_keys)
    return blocks.reshape(ACROSS_FIRST, ACROSS_SECOND, ACROSS_THIRD, DUAL_SIZE, DUAL_SIZE)


def draw_dual_operator(key, part):
    return operator_blocks(jax.random.fold_in(key, 11), 0.7, 1.4)


def draw_dirichlet(key, part):
    return operator_blocks(jax.random.fold_in(key, 12), 0.7, 2.0)


def draw_coarse_inverse(key, part):
    whole = spd_block(jax.random.fold_in(key, 13), COARSE_SIZE, 0.7, 1.4)
    return whole.reshape(ACROSS_FIRST, ACROSS_SECOND, ACROSS_THIRD, GENEO_MODES, COARSE_SIZE)


def pair_tables(key):
    blocks = block_list_drawn()
    starts = {}
    for direction, cursor, extent in blocks:
        starts[direction] = cursor
    grid = (ACROSS_FIRST, ACROSS_SECOND, ACROSS_THIRD)
    device_total = ACROSS_FIRST * ACROSS_SECOND * ACROSS_THIRD
    first_axis = jnp.arange(ACROSS_FIRST)[:, None, None]
    second_axis = jnp.arange(ACROSS_SECOND)[None, :, None]
    third_axis = jnp.arange(ACROSS_THIRD)[None, None, :]

    def inside(direction):
        result = (first_axis + direction[0] >= 0) & (first_axis + direction[0] < ACROSS_FIRST)
        result = result & (second_axis + direction[1] >= 0) & (second_axis + direction[1] < ACROSS_SECOND)
        return result & (third_axis + direction[2] >= 0) & (third_axis + direction[2] < ACROSS_THIRD)
    partners = {}
    sign_parts = {}
    for number, record in enumerate(blocks):
        direction, cursor, extent = record
        leading = [component for component in direction if component != 0][0]
        if leading < 0:
            continue
        opposite = (-direction[0], -direction[1], -direction[2])
        block_key = jax.random.fold_in(key, number)
        perm_keys = jax.random.split(jax.random.fold_in(block_key, 1), device_total)

        def permute(one_key, extent=extent):
            return jax.random.permutation(one_key, extent)
        order_table = jax.vmap(permute)(perm_keys).reshape(grid + (extent,)).astype(jnp.int32)
        sign_table = 2 * jax.random.randint(jax.random.fold_in(block_key, 2), grid + (extent,), 0, 2, jnp.int32) - 1
        spare_sign = 2 * jax.random.randint(jax.random.fold_in(block_key, 3), grid + (extent,), 0, 2, jnp.int32) - 1
        own_index = jnp.arange(extent, dtype=jnp.int32)
        forward = inside(direction)[:, :, :, None]
        partners[direction] = jnp.where(forward, starts[opposite] + order_table, cursor + own_index).astype(jnp.int32)
        sign_parts[direction] = sign_table
        moved_order = jnp.roll(order_table, direction, axis=(0, 1, 2))
        moved_sign = jnp.roll(sign_table, direction, axis=(0, 1, 2))
        inverse = jnp.argsort(moved_order, axis=-1).astype(jnp.int32)
        backward = inside(opposite)[:, :, :, None]
        partners[opposite] = jnp.where(backward, cursor + inverse, starts[opposite] + own_index).astype(jnp.int32)
        sign_parts[opposite] = jnp.where(backward, -jnp.take_along_axis(moved_sign, inverse, axis=-1), spare_sign).astype(jnp.int32)
    partner_all = jnp.concatenate([partners[record[0]] for record in blocks], axis=-1)
    sign_all = jnp.concatenate([sign_parts[record[0]] for record in blocks], axis=-1)
    return (partner_all, sign_all)


def draw_partner_slot(key, part):
    partner_all, sign_all = pair_tables(jax.random.fold_in(key, 23))
    return partner_all


def draw_jump_sign(key, part):
    partner_all, sign_all = pair_tables(jax.random.fold_in(key, 23))
    return sign_all


def draw_mode_count(key, part):
    device_total = ACROSS_FIRST * ACROSS_SECOND * ACROSS_THIRD
    base_key = jax.random.fold_in(key, 31)
    counts = jax.random.randint(base_key, (device_total,), GENEO_MODES // 4, GENEO_MODES + 1, jnp.int32)
    order_list = jax.random.permutation(jax.random.fold_in(base_key, 1), device_total)
    counts = counts.at[order_list[0]].set(GENEO_MODES).at[order_list[1]].set(GENEO_MODES // 4)
    return counts.reshape(ACROSS_FIRST, ACROSS_SECOND, ACROSS_THIRD)


def level_of(own_key, shape, cuts, smallest, largest):
    level = 1.0
    for dim, parts in cuts:
        draws = jax.random.uniform(jax.random.fold_in(jax.random.fold_in(own_key, 6), dim), (parts,), jnp.float32, smallest / len(cuts), largest / len(cuts))
        level = level * jnp.repeat(jnp.exp(draws), shape[dim] // parts).reshape((-1,) + (1,) * (len(shape) - 1 - dim))
    return level


def gaussian(key, shape, scale, limit, shards=(), kind=jnp.bfloat16):
    values = scale * jax.random.normal(key, shape, jnp.float32)
    if shards:
        values = values * level_of(key, shape, shards, -0.22, 0.18)
    return jnp.clip(values, -limit, limit).astype(kind)


def setup_inputs(seed: int = 0) -> dict:
    streams_of = jax.random.split(jax.random.key(seed), 9)
    adjoint_rhs = draw_adjoint_rhs(jax.random.fold_in(streams_of[8], 71), 0)
    dual_operator = draw_dual_operator(jax.random.fold_in(streams_of[8], 71), 0)
    dirichlet = draw_dirichlet(jax.random.fold_in(streams_of[8], 71), 0)
    geneo_modes = gaussian(streams_of[3], (ACROSS_FIRST, ACROSS_SECOND, ACROSS_THIRD, GENEO_MODES, DUAL_SIZE), DUAL_SIZE ** -0.5, 0.1875, ((0, 8), (1, 4), (2, 8)), jnp.float32)
    coarse_inverse = draw_coarse_inverse(jax.random.fold_in(streams_of[8], 71), 0)
    partner_slot = draw_partner_slot(jax.random.fold_in(streams_of[8], 71), 0)
    jump_sign = draw_jump_sign(jax.random.fold_in(streams_of[8], 71), 0)
    mode_count = draw_mode_count(jax.random.fold_in(streams_of[8], 71), 0)
    return dict(adjoint_rhs=adjoint_rhs, dual_operator=dual_operator, dirichlet=dirichlet, geneo_modes=geneo_modes, coarse_inverse=coarse_inverse, partner_slot=partner_slot, jump_sign=jump_sign, mode_count=mode_count)


def block_list():
    blocks = []
    cursor = 0
    for shift_first in (-1, 0, 1):
        for shift_second in (-1, 0, 1):
            for shift_third in (-1, 0, 1):
                nonzero = abs(shift_first) + abs(shift_second) + abs(shift_third)
                if nonzero == 0:
                    continue
                extent = FACE_SLOTS if nonzero == 1 else (EDGE_SLOTS if nonzero == 2 else CORNER_SLOTS)
                blocks.append(((shift_first, shift_second, shift_third), cursor, extent))
                cursor += extent
    return blocks


def paired_mask():
    first_axis = jnp.arange(ACROSS_FIRST)[:, None, None]
    second_axis = jnp.arange(ACROSS_SECOND)[None, :, None]
    third_axis = jnp.arange(ACROSS_THIRD)[None, None, :]
    pieces = []
    for direction, cursor, extent in block_list():
        inside = (first_axis + direction[0] >= 0) & (first_axis + direction[0] < ACROSS_FIRST)
        inside = inside & (second_axis + direction[1] >= 0) & (second_axis + direction[1] < ACROSS_SECOND)
        inside = inside & (third_axis + direction[2] >= 0) & (third_axis + direction[2] < ACROSS_THIRD)
        pieces.append(jnp.broadcast_to(inside[:, :, :, None], (ACROSS_FIRST, ACROSS_SECOND, ACROSS_THIRD, extent)))
    return jnp.concatenate(pieces, axis=-1).astype(jnp.float32)


def assemble(values, partner_slot, paired):
    pieces = []
    for direction, cursor, extent in block_list():
        neighbour = jnp.roll(values, (-direction[0], -direction[1], -direction[2]), axis=(0, 1, 2))
        index_block = partner_slot[:, :, :, None, cursor:cursor + extent].astype(jnp.int32)
        index_block = jnp.broadcast_to(index_block, values.shape[:4] + (extent,))
        pieces.append(jnp.take_along_axis(neighbour, index_block, axis=-1))
    arrived = jnp.concatenate(pieces, axis=-1)
    return values + paired[:, :, :, None, :] * arrived


def reference(adjoint_rhs, dual_operator, dirichlet, geneo_modes, coarse_inverse, partner_slot, jump_sign, mode_count):
    precise_mode = lax.Precision.HIGHEST
    paired = paired_mask()
    weight = (1.0 - 0.5 * paired)[:, :, :, None, :]
    sign_values = jump_sign.astype(jnp.float32)[:, :, :, None, :]
    in_use = (jnp.arange(GENEO_MODES)[None, None, None, :] < mode_count[:, :, :, None]).astype(jnp.float32)
    in_use = in_use[:, :, :, None, :]

    def apply_dual(current):
        mapped = jnp.einsum("abcrm,abcmn->abcrn", sign_values * current, dual_operator, precision=precise_mode)
        return assemble(sign_values * mapped, partner_slot, paired)

    def precondition(current):
        scaled = weight * sign_values
        local_term = scaled * jnp.einsum("abcrm,abcmn->abcrn", scaled * current, dirichlet, precision=precise_mode)
        coeff = jnp.einsum("abcrm,abcjm->abcrj", current, geneo_modes, precision=precise_mode) * in_use
        flat = jnp.transpose(coeff, (3, 0, 1, 2, 4)).reshape(ADJOINT_LOADS, COARSE_SIZE)
        coarse = jnp.einsum("abcjk,rk->abcrj", coarse_inverse, flat, precision=precise_mode) * in_use
        coarse_field = jnp.einsum("abcrj,abcjm->abcrm", coarse, geneo_modes, precision=precise_mode)
        return assemble(local_term + coarse_field, partner_slot, paired)

    def inner(former, latter):
        return jnp.sum(weight * former * latter, axis=(0, 1, 2, 4))

    solution = jnp.zeros_like(adjoint_rhs)
    residual = adjoint_rhs
    preconditioned = precondition(residual)
    direction = preconditioned
    energy = inner(residual, preconditioned)
    for step_number in range(DUAL_STEPS):
        mapped = apply_dual(direction)
        step_size = (energy / inner(direction, mapped))[None, None, None, :, None]
        solution = solution + step_size * direction
        residual = residual - step_size * mapped
        preconditioned = precondition(residual)
        energy_next = inner(residual, preconditioned)
        direction = preconditioned + (energy_next / energy)[None, None, None, :, None] * direction
        energy = energy_next
    return solution, preconditioned
```

```python
import functools

import jax
import jax.numpy as jnp
from jax import lax
from jax.experimental import pallas as pl
from jax.experimental.pallas import tpu as pltpu
from jax.sharding import PartitionSpec as P

FACE_SLOTS = 144
EDGE_SLOTS = 12
CORNER_SLOTS = 2
DUAL_STEPS = 3
LANES = 128
MESH = pl.DeviceIdType.MESH


def block_list():
    blocks = []
    cursor = 0
    for first in (-1, 0, 1):
        for second in (-1, 0, 1):
            for third in (-1, 0, 1):
                nonzero = abs(first) + abs(second) + abs(third)
                if nonzero == 0:
                    continue
                extent = (FACE_SLOTS, EDGE_SLOTS, CORNER_SLOTS)[nonzero - 1]
                blocks.append(((first, second, third), cursor, extent))
                cursor += extent
    return blocks


BLOCKS = block_list()
SPAN = {d: (start, start + extent) for d, start, extent in BLOCKS}


def opposite(d):
    return (-d[0], -d[1], -d[2])


def tiles_of(d):
    start, stop = SPAN[d]
    return start // LANES, (stop - 1) // LANES + 1


def arrival_places():
    places = {}
    cursor = 0
    for d, _, _ in BLOCKS:
        first, last = tiles_of(opposite(d))
        places[d] = cursor
        cursor += last - first
    return places, cursor


PLACES, ARRIVING = arrival_places()


def merge_plan(tile):
    plan = []
    for d, _, _ in sorted(BLOCKS, key=lambda record: SPAN[opposite(record[0])]):
        source = opposite(d)
        first, last = tiles_of(source)
        if first <= tile < last:
            plan.append((min(SPAN[source][1] - tile * LANES, LANES), PLACES[d] + tile - first))
    return plan


def sources_of(tile):
    found = set()
    for d, _, _ in BLOCKS:
        first, last = tiles_of(d)
        if first <= tile < last:
            found.update(range(*tiles_of(opposite(d))))
    return sorted(found)


def in_parts(values):
    leading = values.astype(jnp.bfloat16).astype(jnp.float32)
    return jnp.concatenate([values, values - leading], axis=0).astype(jnp.bfloat16)


def fold_rows(values):
    rows = values.shape[0] // 2
    return values[:rows] + values[rows:]


def product(rows, table):
    parts = in_parts(rows)
    whole = jnp.dot(parts, table[1], preferred_element_type=jnp.float32)
    whole += jnp.dot(parts, table[0], preferred_element_type=jnp.float32)
    return fold_rows(whole)


def contract_last(rows, table):
    whole = lax.dot_general(
        in_parts(rows), table, (((1,), (1,)), ((), ())), preferred_element_type=jnp.float32
    )
    whole = fold_rows(whole)
    half = whole.shape[1] // 2
    return whole[:, :half] + whole[:, half:]


def kernel(
    sizes,
    rhs_hbm,
    dual_hbm,
    dirichlet_hbm,
    modes_hbm,
    coarse_hbm,
    partner_hbm,
    sign_hbm,
    count_ref,
    x_ref,
    z_ref,
    modes,
    partner,
    sign_int,
    stage_dual,
    stage_dirichlet,
    dual,
    dirichlet,
    coarse_line,
    coarse_table,
    modes_send,
    modes_field,
    line_third,
    line_first,
    line_second,
    outgoing,
    arriving,
    residual,
    direction,
    mapped,
    local_residual,
    local_mapped,
    small,
    sign_ref,
    weight_ref,
    lane_ref,
    tile_ref,
    local_sem,
    rows_sem,
    line_send,
    line_recv,
    halo_send,
    halo_recv,
):
    place = (lax.axis_index("gx"), lax.axis_index("gy"), lax.axis_index("gz"))
    loads, order = rhs_hbm.shape
    modes_total = modes_hbm.shape[0]
    span_columns = coarse_line.shape[1] // sizes[0]

    def shifted(shifts):
        return tuple(
            lax.rem(place[i] + shifts[i] + sizes[i], sizes[i]) if shifts[i] else place[i]
            for i in range(3)
        )

    def along(axis, distance):
        shifts = [0, 0, 0]
        shifts[axis] = distance
        return shifted(shifts)

    loading = [
        pltpu.make_async_copy(rhs_hbm, residual, local_sem.at[0]),
        pltpu.make_async_copy(modes_hbm, modes, local_sem.at[1]),
        pltpu.make_async_copy(sign_hbm, sign_int, local_sem.at[2]),
        pltpu.make_async_copy(partner_hbm, partner, local_sem.at[3]),
        pltpu.make_async_copy(dirichlet_hbm, stage_dirichlet, local_sem.at[4]),
        pltpu.make_async_copy(dual_hbm, stage_dual, local_sem.at[5]),
    ]
    for copy in loading:
        copy.start()

    partners = [d for d, _, _ in BLOCKS]
    for axis in range(3):
        for distance in range(2, sizes[axis] - 1):
            shifts = [0, 0, 0]
            shifts[axis] = distance
            partners.append(tuple(shifts))
    barrier = pltpu.get_barrier_semaphore()
    for shifts in partners:
        pl.semaphore_signal(barrier, inc=1, device_id=shifted(shifts), device_id_type=MESH)

    slot = lax.broadcasted_iota(jnp.int32, (loads, order), 1)
    paired = jnp.zeros((loads, order), jnp.int32)
    for d, start, extent in BLOCKS:
        inside = jnp.int32(1)
        for axis in range(3):
            if d[axis] == -1:
                inside = inside * jnp.where(place[axis] > 0, 1, 0)
            if d[axis] == 1:
                inside = inside * jnp.where(place[axis] < sizes[axis] - 1, 1, 0)
        paired = jnp.where((slot >= start) & (slot < start + extent), inside, paired)
    weight_ref[...] = 1.0 - 0.5 * paired.astype(jnp.float32)
    loading[2].wait()
    sign_ref[...] = jnp.broadcast_to(sign_int[...], (loads, order)).astype(jnp.float32)
    loading[3].wait()
    spread = jnp.broadcast_to(partner[...], (loads, order))
    lane_ref[...] = spread & (LANES - 1)
    tile_ref[...] = jnp.where(paired > 0, spread >> 7, -1)

    loading[1].wait()
    row = lax.broadcasted_iota(jnp.int32, (modes_total, order), 0)
    used = jnp.where(row < count_ref[0], modes[...], 0.0)
    leading = used.astype(jnp.bfloat16)
    remaining = (used - leading.astype(jnp.float32)).astype(jnp.bfloat16)
    modes_send[...] = jnp.zeros_like(modes_send)
    modes_field[...] = jnp.zeros_like(modes_field)
    quarter = pl.multiple_of(lax.rem(place[2], 4) * modes_total, modes_total)
    modes_send[pl.ds(quarter, modes_total), :] = leading
    modes_send[pl.ds(LANES + quarter, modes_total), :] = remaining
    own_rows = pl.ds(pl.multiple_of(place[1] * modes_total, modes_total), modes_total)
    modes_field[0, own_rows, :] = leading
    modes_field[1, own_rows, :] = remaining

    loading[0].wait()
    pl.semaphore_wait(barrier, len(partners))

    def line_start(axis, buffer, stage, message):
        buffer[stage, place[axis]] = message
        for distance in range(1, sizes[axis]):
            pltpu.make_async_remote_copy(
                src_ref=buffer.at[stage, place[axis]],
                dst_ref=buffer.at[stage, place[axis]],
                send_sem=line_send.at[stage, axis],
                recv_sem=line_recv.at[stage, axis],
                device_id=along(axis, distance),
                device_id_type=MESH,
            ).start()

    def line_wait(axis, buffer, stage):
        others = buffer.at[stage, pl.ds(0, sizes[axis] - 1)]
        copy = pltpu.make_async_remote_copy(
            src_ref=others,
            dst_ref=others,
            send_sem=line_send.at[stage, axis],
            recv_sem=line_recv.at[stage, axis],
            device_id=along(axis, 1),
            device_id_type=MESH,
        )
        copy.wait_recv()
        copy.wait_send()

    def gather_start(stage, values, sums):
        message = jnp.concatenate([contract_last(values, modes_send[...]), sums], axis=1)
        line_start(2, line_third, stage, message)

    def gather_middle(stage):
        line_wait(2, line_third, stage)
        half = sizes[2] // 2
        groups = []
        sums = jnp.zeros((loads, LANES), jnp.float32)
        for group in range(2):
            total = jnp.zeros((loads, LANES), jnp.float32)
            for number in range(group * half, group * half + half):
                total += line_third[stage, number, :, :LANES]
                sums += line_third[stage, number, :, LANES:]
            groups.append(total)
        line_start(0, line_first, stage, jnp.concatenate(groups + [sums], axis=1))

    def gather_last(stage):
        line_wait(0, line_first, stage)
        pieces = []
        sums = jnp.zeros((loads, LANES), jnp.float32)
        for number in range(sizes[0]):
            pieces.append(line_first[stage, number, :, :span_columns])
            sums += line_first[stage, number, :, span_columns:]
        partial = contract_last(jnp.concatenate(pieces, axis=1), coarse_table[...])
        line_start(1, line_second, stage, jnp.concatenate([partial, sums], axis=1))

    def gather_end(stage):
        line_wait(1, line_second, stage)
        total = line_second[stage, 0]
        for number in range(1, sizes[1]):
            total += line_second[stage, number]
        return total[:, :LANES], total[:, LANES:]

    def halo_start(phase, values):
        outgoing[phase] = values
        for d, _, _ in BLOCKS:
            first, last = tiles_of(d)
            at = PLACES[opposite(d)]
            pltpu.make_async_remote_copy(
                src_ref=outgoing.at[phase, :, pl.ds(first * LANES, (last - first) * LANES)],
                dst_ref=arriving.at[phase, :, pl.ds(at * LANES, (last - first) * LANES)],
                send_sem=halo_send.at[phase],
                recv_sem=halo_recv.at[phase],
                device_id=shifted(d),
                device_id_type=MESH,
            ).start()

    def halo_end(phase):
        copy = pltpu.make_async_remote_copy(
            src_ref=arriving.at[phase],
            dst_ref=arriving.at[phase],
            send_sem=halo_send.at[phase],
            recv_sem=halo_recv.at[phase],
            device_id=shifted(BLOCKS[0][0]),
            device_id_type=MESH,
        )
        copy.wait_recv()
        copy.wait_send()
        lane = lax.broadcasted_iota(jnp.int32, (loads, LANES), 1)
        tiles = []
        for tile in range(order // LANES):
            plan = merge_plan(tile)
            merged = None
            for stop, at in reversed(plan):
                piece = arriving[phase, :, at * LANES : (at + 1) * LANES]
                merged = piece if merged is None else jnp.where(lane < stop, piece, merged)
            tiles.append(merged)
        results = []
        for tile in range(order // LANES):
            here = slice(tile * LANES, (tile + 1) * LANES)
            taken = jnp.zeros((loads, LANES), jnp.float32)
            for source in sources_of(tile):
                moved = jnp.take_along_axis(
                    tiles[source], lane_ref[:, here], axis=1, mode="promise_in_bounds"
                )
                taken = jnp.where(tile_ref[:, here] == source, moved, taken)
            results.append(outgoing[phase, :, here] + taken)
        return jnp.concatenate(results, axis=1)

    def local_term(values):
        scaled = weight_ref[...] * sign_ref[...]
        return scaled * product(scaled * values, dirichlet)

    def split_table(source, table):
        step = 64

        def body(i, carry):
            rows = pl.ds(pl.multiple_of(i * step, step), step)
            values = source[rows, :]
            leading = values.astype(jnp.bfloat16)
            table[0, rows, :] = leading
            table[1, rows, :] = (values - leading.astype(jnp.float32)).astype(jnp.bfloat16)
            return carry

        lax.fori_loop(0, order // step, body, 0)

    def inner(former, latter):
        whole = weight_ref[...] * former * latter
        total = whole[:, :LANES]
        for tile in range(1, order // LANES):
            total += whole[:, tile * LANES : (tile + 1) * LANES]
        return jnp.sum(total, axis=1, keepdims=True)

    def in_lanes(columns):
        lane = lax.broadcasted_iota(jnp.int32, (loads, LANES), 1)
        tile = jnp.zeros((loads, LANES), jnp.float32)
        for number, column in enumerate(columns):
            tile = jnp.where(lane == number, column, tile)
        return tile

    gather_start(0, residual[...], jnp.zeros((loads, LANES), jnp.float32))

    def rows_copy(first, target, peer):
        source = coarse_hbm.at[
            :, pl.ds(pl.multiple_of((first * sizes[1] + target) * span_columns, span_columns), span_columns)
        ]
        goal = coarse_line.at[
            pl.ds(pl.multiple_of(place[1] * modes_total, modes_total), modes_total),
            pl.ds(pl.multiple_of(first * span_columns, span_columns), span_columns),
        ]
        if peer is None:
            return pltpu.make_async_copy(source, goal, local_sem.at[6])
        return pltpu.make_async_remote_copy(
            src_ref=source,
            dst_ref=goal,
            send_sem=rows_sem.at[0],
            recv_sem=rows_sem.at[1],
            device_id=peer,
            device_id_type=MESH,
        )

    for distance in range(1, sizes[1]):
        peer = along(1, distance)

        def send_rows(first, carry, peer=peer):
            rows_copy(first, peer[1], peer).start()
            return carry

        lax.fori_loop(0, sizes[0], send_rows, 0)

    def keep_rows(first, carry):
        rows_copy(first, place[1], None).start()
        return carry

    lax.fori_loop(0, sizes[0], keep_rows, 0)

    loading[4].wait()
    split_table(stage_dirichlet, dirichlet)
    gather_middle(0)
    local_residual[...] = local_term(residual[...])
    loading[5].wait()
    split_table(stage_dual, dual)

    others = coarse_line.at[pl.ds(0, (sizes[1] - 1) * modes_total), :]
    rows_wait = pltpu.make_async_remote_copy(
        src_ref=others,
        dst_ref=others,
        send_sem=rows_sem.at[0],
        recv_sem=rows_sem.at[1],
        device_id=along(1, 1),
        device_id_type=MESH,
    )
    rows_wait.wait_recv()
    rows_wait.wait_send()
    own = coarse_line.at[pl.ds(0, modes_total), :]
    pltpu.make_async_copy(own, own, local_sem.at[6]).wait()
    rows = coarse_line[...]
    leading = rows.astype(jnp.bfloat16)
    coarse_table[:LANES, :] = leading
    coarse_table[LANES:, :] = (rows - leading.astype(jnp.float32)).astype(jnp.bfloat16)

    gather_last(0)
    zeros = jnp.zeros((loads, order), jnp.float32)
    direction[...] = zeros
    mapped[...] = zeros
    local_mapped[...] = zeros
    x_ref[...] = zeros
    coarse, _ = gather_end(0)
    small[0] = coarse
    small[1] = jnp.zeros((loads, LANES), jnp.float32)
    small[2] = jnp.ones((loads, LANES), jnp.float32)
    halo_start(0, local_residual[...] + product(coarse, modes_field))
    z_ref[...] = halo_end(0)

    def step(number, carry):
        stage = number + 1
        image = 2 * number + 1
        sign = sign_ref[...]
        conditioned = z_ref[...]
        halo_start(image, sign * product(sign * conditioned, dual))
        energy_part = inner(residual[...], conditioned)
        cross_part = inner(conditioned, mapped[...])
        fresh = halo_end(image)
        curve_part = inner(conditioned, fresh)
        other_part = inner(direction[...], fresh)
        gather_start(stage, fresh, in_lanes([energy_part, cross_part, curve_part, other_part]))
        fresh_local = local_term(fresh)
        gather_middle(stage)
        gather_last(stage)
        fresh_coarse, sums = gather_end(stage)

        energy = sums[:, 0:1]
        energy_before = small[2, :, 0:1]
        curve_before = small[2, :, 1:2]
        beta = jnp.where(number == 0, 0.0, energy / energy_before)
        curve = sums[:, 2:3] + beta * (sums[:, 1:2] + sums[:, 3:4]) + beta * beta * curve_before
        alpha = energy / curve
        small[2] = in_lanes([energy, curve])

        coarse_mapped = fresh_coarse + beta * small[1]
        coarse_residual = small[0] - alpha * coarse_mapped
        small[1] = coarse_mapped
        small[0] = coarse_residual
        local_image = fresh_local + beta * local_mapped[...]
        local_mapped[...] = local_image
        local_now = local_residual[...] - alpha * local_image
        local_residual[...] = local_now
        halo_start(image + 1, local_now + product(coarse_residual, modes_field))

        along_now = conditioned + beta * direction[...]
        direction[...] = along_now
        mapped_now = fresh + beta * mapped[...]
        mapped[...] = mapped_now
        x_ref[...] = x_ref[...] + alpha * along_now
        residual[...] = residual[...] - alpha * mapped_now
        z_ref[...] = halo_end(image + 1)
        return carry

    lax.fori_loop(0, DUAL_STEPS, step, 0)


def body(
    sizes,
    adjoint_rhs,
    dual_operator,
    dirichlet,
    geneo_modes,
    coarse_inverse,
    partner_slot,
    jump_sign,
    mode_count,
):
    loads, order = adjoint_rhs.shape[3:]
    modes_total, coarse_size = coarse_inverse.shape[3:]
    columns = coarse_size // sizes[1]
    stages = DUAL_STEPS + 1
    phases = 2 * DUAL_STEPS + 1
    vector = pltpu.VMEM((loads, order), jnp.float32)
    whole = jax.ShapeDtypeStruct((loads, order), jnp.float32)

    def run(*args):

        return pl.pallas_call(
            functools.partial(kernel, sizes),
            out_shape=(whole, whole),
            in_specs=[pl.BlockSpec(memory_space=pl.ANY)] * 7
            + [pl.BlockSpec(memory_space=pltpu.SMEM)],
            out_specs=(
                pl.BlockSpec(memory_space=pltpu.VMEM),
                pl.BlockSpec(memory_space=pltpu.VMEM),
            ),
            scratch_shapes=[
                pltpu.VMEM((modes_total, order), jnp.float32),
                pltpu.VMEM((1, order), jnp.int32),
                pltpu.VMEM((1, order), jnp.int32),
                pltpu.VMEM((order, order), jnp.float32),
                pltpu.VMEM((order, order), jnp.float32),
                pltpu.VMEM((2, order, order), jnp.bfloat16),
                pltpu.VMEM((2, order, order), jnp.bfloat16),
                pltpu.VMEM((LANES, columns), jnp.float32),
                pltpu.VMEM((2 * LANES, columns), jnp.bfloat16),
                pltpu.VMEM((2 * LANES, order), jnp.bfloat16),
                pltpu.VMEM((2, LANES, order), jnp.bfloat16),
                pltpu.VMEM((stages, sizes[2], loads, 2 * LANES), jnp.float32),
                pltpu.VMEM((stages, sizes[0], loads, 3 * LANES), jnp.float32),
                pltpu.VMEM((stages, sizes[1], loads, 2 * LANES), jnp.float32),
                pltpu.VMEM((phases, loads, order), jnp.float32),
                pltpu.VMEM((phases, loads, ARRIVING * LANES), jnp.float32),
                vector,
                vector,
                vector,
                vector,
                vector,
                pltpu.VMEM((3, loads, LANES), jnp.float32),
                vector,
                vector,
                pltpu.VMEM((loads, order), jnp.int32),
                pltpu.VMEM((loads, order), jnp.int32),
                pltpu.SemaphoreType.DMA((7,)),
                pltpu.SemaphoreType.DMA((2,)),
                pltpu.SemaphoreType.DMA((stages, 3)),
                pltpu.SemaphoreType.DMA((stages, 3)),
                pltpu.SemaphoreType.DMA((phases,)),
                pltpu.SemaphoreType.DMA((phases,)),
            ],
            compiler_params=pltpu.CompilerParams(
                collective_id=0, has_side_effects=True, vmem_limit_bytes=56 * 1024 * 1024
            ),
        )(*args)

    found, force = run(
        adjoint_rhs.reshape(loads, order),
        dual_operator.reshape(order, order),
        dirichlet.reshape(order, order),
        geneo_modes.reshape(modes_total, order),
        coarse_inverse.reshape(modes_total, coarse_size),
        partner_slot.reshape(1, order),
        jump_sign.reshape(1, order),
        mode_count.reshape(1),
    )
    return found.reshape(adjoint_rhs.shape), force.reshape(adjoint_rhs.shape)


def solution(mesh):

    sizes = (mesh.shape["gx"], mesh.shape["gy"], mesh.shape["gz"])
    spot = ("gx", "gy", "gz")
    placed = (
        P(*spot, None, None),
        P(*spot, None, None),
        P(*spot, None, None),
        P(*spot, None, None),
        P(*spot, None, None),
        P(*spot, None),
        P(*spot, None),
        P(*spot),
    )
    return jax.shard_map(
        functools.partial(body, sizes),
        mesh=mesh,
        in_specs=placed,
        out_specs=(P(*spot, None, None), P(*spot, None, None)),
        check_vma=False,
    )
```

```python
import functools

import jax
import jax.numpy as jnp
from jax import lax
from jax.experimental import pallas as pl
from jax.experimental.pallas import tpu as pltpu
from jax.sharding import PartitionSpec as P

FACE_SLOTS = 144
EDGE_SLOTS = 12
CORNER_SLOTS = 2
DUAL_STEPS = 3
LANES = 128
MESH = pl.DeviceIdType.MESH


def block_list():
    blocks = []
    cursor = 0
    for first in (-1, 0, 1):
        for second in (-1, 0, 1):
            for third in (-1, 0, 1):
                nonzero = abs(first) + abs(second) + abs(third)
                if nonzero == 0:
                    continue
                extent = (FACE_SLOTS, EDGE_SLOTS, CORNER_SLOTS)[nonzero - 1]
                blocks.append(((first, second, third), cursor, extent))
                cursor += extent
    return blocks


BLOCKS = block_list()
FAR_FIRST = sorted((record[0] for record in BLOCKS), key=lambda d: -sum(map(abs, d)))
SPAN = {d: (start, start + extent) for d, start, extent in BLOCKS}


def opposite(d):
    return (-d[0], -d[1], -d[2])


def tiles_of(d):
    start, stop = SPAN[d]
    return start // LANES, (stop - 1) // LANES + 1


def arrival_places():
    places = {}
    cursor = 0
    for d, _, _ in BLOCKS:
        first, last = tiles_of(opposite(d))
        places[d] = cursor
        cursor += last - first
    return places, cursor


PLACES, ARRIVING = arrival_places()


def merge_plan(tile):
    plan = []
    for d, _, _ in sorted(BLOCKS, key=lambda record: SPAN[opposite(record[0])]):
        source = opposite(d)
        first, last = tiles_of(source)
        if first <= tile < last:
            plan.append((min(SPAN[source][1] - tile * LANES, LANES), PLACES[d] + tile - first))
    return plan


def sources_of(tile):
    found = set()
    for d, _, _ in BLOCKS:
        first, last = tiles_of(d)
        if first <= tile < last:
            found.update(range(*tiles_of(opposite(d))))
    return sorted(found)


def in_parts(values):
    leading = values.astype(jnp.bfloat16).astype(jnp.float32)
    return jnp.concatenate([values, values - leading], axis=0).astype(jnp.bfloat16)


def fold_rows(values):
    rows = values.shape[0] // 2
    return values[:rows] + values[rows:]


def product(rows, table):
    parts = in_parts(rows)
    whole = jnp.dot(parts, table[1], preferred_element_type=jnp.float32)
    whole += jnp.dot(parts, table[0], preferred_element_type=jnp.float32)
    return fold_rows(whole)


def contract_last(rows, table):
    whole = lax.dot_general(
        in_parts(rows), table, (((1,), (1,)), ((), ())), preferred_element_type=jnp.float32
    )
    whole = fold_rows(whole)
    half = whole.shape[1] // 2
    return whole[:, :half] + whole[:, half:]


def kernel(
    sizes,
    rhs_hbm,
    dual_hbm,
    dirichlet_hbm,
    modes_hbm,
    coarse_hbm,
    partner_hbm,
    sign_hbm,
    count_hbm,
    both,
    modes,
    partner,
    sign_int,
    count,
    stage_dual,
    stage_dirichlet,
    dual,
    dirichlet,
    coarse_line,
    coarse_table,
    modes_send,
    modes_field,
    given,
    taken_in,
    shared,
    shared_in,
    outgoing,
    arriving,
    residual,
    direction,
    mapped,
    local_residual,
    local_mapped,
    small,
    sign_ref,
    weight_ref,
    lane_ref,
    tile_ref,
    local_sem,
    rows_send,
    rows_recv,
    take_send,
    take_recv,
    share_send,
    share_recv,
    halo_send,
    halo_recv,
):
    place = (lax.axis_index("gx"), lax.axis_index("gy"), lax.axis_index("gz"))
    loads, order = rhs_hbm.shape
    x_ref, z_ref = both.at[0], both.at[1]
    modes_total = modes_hbm.shape[0]
    half = sizes[2] // 2
    core = lax.rem(place[2], 2)
    chip = place[2] // 2
    side = place[2] // half
    pack = LANES // modes_total

    def shifted(shifts):
        return tuple(
            lax.rem(place[i] + shifts[i] + sizes[i], sizes[i]) if shifts[i] else place[i]
            for i in range(3)
        )

    def ring(distance, size):
        return min(distance, size - distance)

    takers = sorted(
        ((first, hop) for first in range(sizes[0]) for hop in range(half)),
        key=lambda pair: -ring(pair[0], sizes[0]) - ring(pair[1], half),
    )[:-1]
    sharers = sorted(
        ((second, other) for second in range(sizes[1]) for other in range(2)),
        key=lambda pair: -2 * ring(pair[0], sizes[1]) - pair[1],
    )[:-1]

    def taker(first, hop):
        return (
            lax.rem(place[0] + first, sizes[0]),
            place[1],
            2 * lax.rem(chip + hop, half) + side,
        )

    def sharer(second, other):
        third = 2 * chip + (1 - core) if other else place[2]
        return (place[0], lax.rem(place[1] + second, sizes[1]), third)

    sibling = sharer(0, 1)
    keeps = core == side

    loading = [
        pltpu.make_async_copy(rhs_hbm, residual, local_sem.at[0]),
        pltpu.make_async_copy(modes_hbm, modes, local_sem.at[1]),
        pltpu.make_async_copy(sign_hbm, sign_int, local_sem.at[2]),
        pltpu.make_async_copy(partner_hbm, partner, local_sem.at[3]),
        pltpu.make_async_copy(dirichlet_hbm, stage_dirichlet, local_sem.at[4]),
        pltpu.make_async_copy(dual_hbm, stage_dual, local_sem.at[5]),
        pltpu.make_async_copy(count_hbm, count, local_sem.at[7]),
    ]
    for copy in loading:
        copy.start()

    barrier = pltpu.get_barrier_semaphore()
    greeted = 0
    for d in FAR_FIRST:
        pl.semaphore_signal(barrier, inc=1, device_id=shifted(d), device_id_type=MESH)
        greeted += 1
    def greet_giver(first, hop):
        third = half * core + lax.rem(place[2] + hop, half)
        giver = (lax.rem(place[0] + first, sizes[0]), place[1], third)
        pl.semaphore_signal(barrier, inc=1, device_id=giver, device_id_type=MESH)

    for first, hop in takers:
        greet_giver(first, hop)
        greeted += 1

    @pl.when(jnp.logical_not(keeps))
    def _():
        greet_giver(0, 0)

    for second, other in sharers:
        pl.semaphore_signal(
            barrier, inc=1, device_id=sharer(second, other), device_id_type=MESH
        )
        greeted += 1

    slot = lax.broadcasted_iota(jnp.int32, (loads, order), 1)
    paired = jnp.zeros((loads, order), jnp.int32)
    for d, start, extent in BLOCKS:
        inside = jnp.int32(1)
        for axis in range(3):
            if d[axis] == -1:
                inside = inside * jnp.where(place[axis] > 0, 1, 0)
            if d[axis] == 1:
                inside = inside * jnp.where(place[axis] < sizes[axis] - 1, 1, 0)
        paired = jnp.where((slot >= start) & (slot < start + extent), inside, paired)
    weight_ref[...] = 1.0 - 0.5 * paired.astype(jnp.float32)
    loading[2].wait()
    sign_ref[...] = jnp.broadcast_to(sign_int[...], (loads, order)).astype(jnp.float32)
    loading[3].wait()
    spread = jnp.broadcast_to(partner[...], (loads, order))
    lane_ref[...] = spread & (LANES - 1)
    tile_ref[...] = jnp.where(paired > 0, spread >> 7, -1)

    loading[1].wait()
    loading[6].wait()
    row = lax.broadcasted_iota(jnp.int32, (modes_total, order), 0)
    used = jnp.where(row < count[0, 0], modes[...], 0.0)
    leading = used.astype(jnp.bfloat16)
    remaining = (used - leading.astype(jnp.float32)).astype(jnp.bfloat16)
    modes_send[...] = jnp.zeros_like(modes_send)
    modes_field[...] = jnp.zeros_like(modes_field)
    spare = lax.rem(place[2] + 1, pack) * modes_total
    quarter = pl.multiple_of(lax.rem(place[2], pack) * modes_total, modes_total)
    modes_send[pl.ds(quarter, modes_total), :] = leading
    modes_send[pl.ds(LANES + quarter, modes_total), :] = remaining
    own_rows = pl.ds(pl.multiple_of(place[1] * modes_total, modes_total), modes_total)
    modes_field[0, own_rows, :] = leading
    modes_field[1, own_rows, :] = remaining

    loading[0].wait()
    pl.semaphore_wait(barrier, greeted + jnp.where(keeps, 0, 1))

    def remote(source, goal, sems, index, peer):
        return pltpu.make_async_remote_copy(
            src_ref=source,
            dst_ref=goal,
            send_sem=sems[0].at[index],
            recv_sem=sems[1].at[index],
            device_id=peer,
            device_id_type=MESH,
        )

    def wait_for(buffer, sems, index):
        copy = remote(buffer, buffer, sems, index, sibling)
        copy.wait_recv()
        copy.wait_send()

    take_sems = (take_send, take_recv)
    share_sems = (share_send, share_recv)

    def gather_start(stage, values, sums):
        message = contract_last(values, modes_send[...]) + in_lanes(sums, spare)
        own = place[0] * half + lax.rem(place[2], half)
        given[stage] = message

        def give(peer):
            remote(given.at[stage], taken_in.at[stage, own], take_sems, stage, peer).start()

        for first, hop in takers:
            give(taker(first, hop))

        @pl.when(keeps)
        def _():
            taken_in[stage, own] = message

        @pl.when(jnp.logical_not(keeps))
        def _():
            give(sibling)

    def gather_middle(stage):
        count = sizes[0] * half

        @pl.when(keeps)
        def _():
            wait_for(taken_in.at[stage, pl.ds(0, count - 1)], take_sems, stage)

        @pl.when(jnp.logical_not(keeps))
        def _():
            wait_for(taken_in.at[stage, pl.ds(0, count)], take_sems, stage)

        pieces = []
        held = [None] * half
        lane = lax.broadcasted_iota(jnp.int32, (loads, LANES), 1)
        sums = jnp.zeros((loads, LANES), jnp.float32)
        for first in range(sizes[0]):
            total = None
            for number in range(half):
                piece = taken_in[stage, first * half + number]
                total = piece if number == 0 else jnp.where(lane < number * modes_total, total, piece)
                held[number] = piece if first == 0 else held[number] + piece
            pieces.append(total)
        for number in range(half):
            start = (number + 1) % pack * modes_total
            inside = (lane >= start) & (lane < start + modes_total)
            sums += jnp.where(inside, held[number], 0.0)
        partial = contract_last(jnp.concatenate(pieces, axis=1), coarse_table[...])
        message = jnp.concatenate([partial[:, :LANES], sums, partial[:, LANES:], sums], axis=1)
        shared[stage] = message
        own = core * sizes[1] + place[1]
        for second, other in sharers:
            mine = (1 - core) if other else core
            part = pl.ds(pl.multiple_of(mine * 2 * LANES, 2 * LANES), 2 * LANES)
            remote(
                shared.at[stage, :, part],
                shared_in.at[stage, own],
                share_sems,
                stage,
                sharer(second, other),
            ).start()
        shared_in[stage, own] = jnp.where(core == 0, message[:, : 2 * LANES], message[:, 2 * LANES :])

    def gather_end(stage):
        count = 2 * sizes[1]
        wait_for(shared_in.at[stage, pl.ds(0, count - 1)], share_sems, stage)
        total = shared_in[stage, 0]
        for number in range(1, count):
            total += shared_in[stage, number]
        sums = total[:, LANES:]
        sums = sums + pltpu.roll(sums, LANES // 2, 1)
        return total[:, :LANES], sums + pltpu.roll(sums, LANES // 4, 1)

    def halo_start(phase, values):
        outgoing[phase] = values
        for d in FAR_FIRST:
            first, last = tiles_of(d)
            at = PLACES[opposite(d)]
            pltpu.make_async_remote_copy(
                src_ref=outgoing.at[phase, :, pl.ds(first * LANES, (last - first) * LANES)],
                dst_ref=arriving.at[phase, :, pl.ds(at * LANES, (last - first) * LANES)],
                send_sem=halo_send.at[phase],
                recv_sem=halo_recv.at[phase],
                device_id=shifted(d),
                device_id_type=MESH,
            ).start()

    def halo_end(phase):
        copy = pltpu.make_async_remote_copy(
            src_ref=arriving.at[phase],
            dst_ref=arriving.at[phase],
            send_sem=halo_send.at[phase],
            recv_sem=halo_recv.at[phase],
            device_id=shifted(BLOCKS[0][0]),
            device_id_type=MESH,
        )
        copy.wait_recv()
        copy.wait_send()
        lane = lax.broadcasted_iota(jnp.int32, (loads, LANES), 1)
        tiles = []
        for tile in range(order // LANES):
            plan = merge_plan(tile)
            merged = None
            for stop, at in reversed(plan):
                piece = arriving[phase, :, at * LANES : (at + 1) * LANES]
                merged = piece if merged is None else jnp.where(lane < stop, piece, merged)
            tiles.append(merged)
        results = []
        for tile in range(order // LANES):
            here = slice(tile * LANES, (tile + 1) * LANES)
            taken = jnp.zeros((loads, LANES), jnp.float32)
            for source in sources_of(tile):
                moved = jnp.take_along_axis(
                    tiles[source], lane_ref[:, here], axis=1, mode="promise_in_bounds"
                )
                taken = jnp.where(tile_ref[:, here] == source, moved, taken)
            results.append(outgoing[phase, :, here] + taken)
        return jnp.concatenate(results, axis=1)

    def local_term(values):
        scaled = weight_ref[...] * sign_ref[...]
        return scaled * product(scaled * values, dirichlet)

    def split_table(source, table):
        step = 64

        def body(i, carry):
            rows = pl.ds(pl.multiple_of(i * step, step), step)
            values = source[rows, :]
            leading = values.astype(jnp.bfloat16)
            table[0, rows, :] = leading
            table[1, rows, :] = (values - leading.astype(jnp.float32)).astype(jnp.bfloat16)
            return carry

        lax.fori_loop(0, order // step, body, 0)

    def inner(former, latter):
        whole = weight_ref[...] * former * latter
        total = whole[:, :LANES]
        for tile in range(1, order // LANES):
            total += whole[:, tile * LANES : (tile + 1) * LANES]
        return jnp.sum(total, axis=1, keepdims=True)

    def in_lanes(columns, start=0):
        lane = lax.broadcasted_iota(jnp.int32, (loads, LANES), 1) - start
        tile = jnp.zeros((loads, LANES), jnp.float32)
        for number, column in enumerate(columns):
            tile = jnp.where(lane == number, column, tile)
        return tile

    gather_start(0, residual[...], [])

    own_place = pl.ds(
        pl.multiple_of(core * LANES + place[1] * modes_total, modes_total), modes_total
    )

    def rows_of(first, second, end):
        start = ((first * sizes[1] + second) * 2 + end) * LANES
        source = coarse_hbm.at[:, pl.ds(pl.multiple_of(start, LANES), LANES)]
        goal = coarse_line.at[own_place, pl.ds(pl.multiple_of(first * LANES, LANES), LANES)]
        return source, goal

    rows_sems = (rows_send, rows_recv)
    for second, other in sharers:
        peer = sharer(second, other)

        def send_rows(first, carry, peer=peer, other=other):
            source, goal = rows_of(first, peer[1], (1 - core) if other else core)
            remote(source, goal, rows_sems, 0, peer).start()
            return carry

        lax.fori_loop(0, sizes[0], send_rows, 0)

    def keep_rows(first, carry):
        source, goal = rows_of(first, place[1], core)
        pltpu.make_async_copy(source, goal, local_sem.at[6]).start()
        return carry

    lax.fori_loop(0, sizes[0], keep_rows, 0)

    loading[4].wait()
    split_table(stage_dirichlet, dirichlet)
    local_residual[...] = local_term(residual[...])
    loading[5].wait()
    split_table(stage_dual, dual)

    rows_total = coarse_line.shape[0]
    wait_for(coarse_line.at[pl.ds(0, rows_total - modes_total), :], rows_sems, 0)
    own = coarse_line.at[pl.ds(0, modes_total), :]
    pltpu.make_async_copy(own, own, local_sem.at[6]).wait()
    rows = coarse_line[...]
    leading = rows.astype(jnp.bfloat16)
    coarse_table[:rows_total, :] = leading
    coarse_table[rows_total:, :] = (rows - leading.astype(jnp.float32)).astype(jnp.bfloat16)

    gather_middle(0)
    zeros = jnp.zeros((loads, order), jnp.float32)
    direction[...] = zeros
    mapped[...] = zeros
    local_mapped[...] = zeros
    x_ref[...] = zeros
    coarse, _ = gather_end(0)
    small[0] = coarse
    small[1] = jnp.zeros((loads, LANES), jnp.float32)
    small[2] = jnp.ones((loads, LANES), jnp.float32)
    halo_start(0, local_residual[...] + product(coarse, modes_field))
    z_ref[...] = halo_end(0)

    def step(number, carry):
        stage = number + 1
        image = 2 * number + 1
        sign = sign_ref[...]
        conditioned = z_ref[...]
        halo_start(image, sign * product(sign * conditioned, dual))
        energy_part = inner(residual[...], conditioned)
        cross_part = inner(conditioned, mapped[...])
        fresh = halo_end(image)
        curve_part = inner(conditioned, fresh)
        other_part = inner(direction[...], fresh)
        gather_start(stage, fresh, [energy_part, cross_part, curve_part, other_part])
        fresh_local = local_term(fresh)
        gather_middle(stage)
        fresh_coarse, sums = gather_end(stage)

        energy = sums[:, 0:1]
        energy_before = small[2, :, 0:1]
        curve_before = small[2, :, 1:2]
        beta = jnp.where(number == 0, 0.0, energy / energy_before)
        curve = sums[:, 2:3] + beta * (sums[:, 1:2] + sums[:, 3:4]) + beta * beta * curve_before
        alpha = energy / curve
        small[2] = in_lanes([energy, curve])

        coarse_mapped = fresh_coarse + beta * small[1]
        coarse_residual = small[0] - alpha * coarse_mapped
        small[1] = coarse_mapped
        small[0] = coarse_residual
        local_image = fresh_local + beta * local_mapped[...]
        local_mapped[...] = local_image
        local_now = local_residual[...] - alpha * local_image
        local_residual[...] = local_now
        halo_start(image + 1, local_now + product(coarse_residual, modes_field))

        along_now = conditioned + beta * direction[...]
        direction[...] = along_now
        mapped_now = fresh + beta * mapped[...]
        mapped[...] = mapped_now
        x_ref[...] = x_ref[...] + alpha * along_now
        residual[...] = residual[...] - alpha * mapped_now
        z_ref[...] = halo_end(image + 1)
        return carry

    lax.fori_loop(0, DUAL_STEPS, step, 0)


def body(
    sizes,
    adjoint_rhs,
    dual_operator,
    dirichlet,
    geneo_modes,
    coarse_inverse,
    partner_slot,
    jump_sign,
    mode_count,
):
    loads, order = adjoint_rhs.shape[3:]
    modes_total, coarse_size = coarse_inverse.shape[3:]
    rows_total = 2 * sizes[1] * modes_total
    columns = coarse_size // (2 * sizes[1])
    stages = DUAL_STEPS + 1
    phases = 2 * DUAL_STEPS + 1
    vector = pltpu.VMEM((loads, order), jnp.float32)
    whole = jax.ShapeDtypeStruct((loads, order), jnp.float32)

    def run(*args):

        return pl.pallas_call(
            functools.partial(kernel, sizes),
            out_shape=jax.ShapeDtypeStruct((2, loads, order), jnp.float32),
            in_specs=[pl.BlockSpec(memory_space=pl.ANY)] * 8,
            out_specs=pl.BlockSpec(memory_space=pltpu.VMEM),
            scratch_shapes=[
                pltpu.VMEM((modes_total, order), jnp.float32),
                pltpu.VMEM((1, order), jnp.int32),
                pltpu.VMEM((1, order), jnp.int32),
                pltpu.SMEM((1, 1), jnp.int32),
                pltpu.VMEM((order, order), jnp.float32),
                pltpu.VMEM((order, order), jnp.float32),
                pltpu.VMEM((2, order, order), jnp.bfloat16),
                pltpu.VMEM((2, order, order), jnp.bfloat16),
                pltpu.VMEM((rows_total, columns), jnp.float32),
                pltpu.VMEM((2 * rows_total, columns), jnp.bfloat16),
                pltpu.VMEM((2 * LANES, order), jnp.bfloat16),
                pltpu.VMEM((2, LANES, order), jnp.bfloat16),
                pltpu.VMEM((stages, loads, LANES), jnp.float32),
                pltpu.VMEM((stages, sizes[0] * sizes[2] // 2, loads, LANES), jnp.float32),
                pltpu.VMEM((stages, loads, 4 * LANES), jnp.float32),
                pltpu.VMEM((stages, 2 * sizes[1], loads, 2 * LANES), jnp.float32),
                pltpu.VMEM((phases, loads, order), jnp.float32),
                pltpu.VMEM((phases, loads, ARRIVING * LANES), jnp.float32),
                vector,
                vector,
                vector,
                vector,
                vector,
                pltpu.VMEM((3, loads, LANES), jnp.float32),
                vector,
                vector,
                pltpu.VMEM((loads, order), jnp.int32),
                pltpu.VMEM((loads, order), jnp.int32),
                pltpu.SemaphoreType.DMA((8,)),
                pltpu.SemaphoreType.DMA((1,)),
                pltpu.SemaphoreType.DMA((1,)),
                pltpu.SemaphoreType.DMA((stages,)),
                pltpu.SemaphoreType.DMA((stages,)),
                pltpu.SemaphoreType.DMA((stages,)),
                pltpu.SemaphoreType.DMA((stages,)),
                pltpu.SemaphoreType.DMA((phases,)),
                pltpu.SemaphoreType.DMA((phases,)),
            ],
            compiler_params=pltpu.CompilerParams(
                collective_id=0, has_side_effects=True, vmem_limit_bytes=56 * 1024 * 1024
            ),
        )(*args)

    both = run(
        adjoint_rhs.reshape(loads, order),
        dual_operator.reshape(order, order),
        dirichlet.reshape(order, order),
        geneo_modes.reshape(modes_total, order),
        coarse_inverse.reshape(modes_total, coarse_size),
        partner_slot.reshape(1, order),
        jump_sign.reshape(1, order),
        mode_count.reshape(1, 1),
    )
    found, force = both[0], both[1]
    return found.reshape(adjoint_rhs.shape), force.reshape(adjoint_rhs.shape)


def solution(mesh):

    sizes = (mesh.shape["gx"], mesh.shape["gy"], mesh.shape["gz"])
    spot = ("gx", "gy", "gz")
    placed = (
        P(*spot, None, None),
        P(*spot, None, None),
        P(*spot, None, None),
        P(*spot, None, None),
        P(*spot, None, None),
        P(*spot, None),
        P(*spot, None),
        P(*spot),
    )
    return jax.shard_map(
        functools.partial(body, sizes),
        mesh=mesh,
        in_specs=placed,
        out_specs=(P(*spot, None, None), P(*spot, None, None)),
        check_vma=False,
    )
```

```python
import functools

import jax
import jax.numpy as jnp
from jax import lax
from jax.experimental import pallas as pl
from jax.experimental.pallas import tpu as pltpu
from jax.sharding import PartitionSpec as P

FACE_SLOTS = 144
EDGE_SLOTS = 12
CORNER_SLOTS = 2
DUAL_STEPS = 3
LANES = 128
MESH = pl.DeviceIdType.MESH


def block_list():
    blocks = []
    cursor = 0
    for first in (-1, 0, 1):
        for second in (-1, 0, 1):
            for third in (-1, 0, 1):
                nonzero = abs(first) + abs(second) + abs(third)
                if nonzero == 0:
                    continue
                extent = (FACE_SLOTS, EDGE_SLOTS, CORNER_SLOTS)[nonzero - 1]
                blocks.append(((first, second, third), cursor, extent))
                cursor += extent
    return blocks


BLOCKS = block_list()
FAR_FIRST = sorted((record[0] for record in BLOCKS), key=lambda d: -sum(map(abs, d)))
SPAN = {d: (start, start + extent) for d, start, extent in BLOCKS}


def opposite(d):
    return (-d[0], -d[1], -d[2])


def tiles_of(d):
    start, stop = SPAN[d]
    return start // LANES, (stop - 1) // LANES + 1


def arrival_places():
    places = {}
    cursor = 0
    for d, _, _ in BLOCKS:
        first, last = tiles_of(opposite(d))
        places[d] = cursor
        cursor += last - first
    return places, cursor


PLACES, ARRIVING = arrival_places()


def merge_plan(tile):
    plan = []
    for d, _, _ in sorted(BLOCKS, key=lambda record: SPAN[opposite(record[0])]):
        source = opposite(d)
        first, last = tiles_of(source)
        if first <= tile < last:
            plan.append((min(SPAN[source][1] - tile * LANES, LANES), PLACES[d] + tile - first))
    return plan


def sources_of(tile):
    found = set()
    for d, _, _ in BLOCKS:
        first, last = tiles_of(d)
        if first <= tile < last:
            found.update(range(*tiles_of(opposite(d))))
    return sorted(found)


def in_parts(values):
    leading = values.astype(jnp.bfloat16).astype(jnp.float32)
    return jnp.concatenate([values, values - leading], axis=0).astype(jnp.bfloat16)


def fold_rows(values):
    rows = values.shape[0] // 2
    return values[:rows] + values[rows:]


def product(rows, table, start=0):
    parts = in_parts(rows)
    here = slice(start, start + rows.shape[1])
    whole = jnp.dot(parts, table[1, here], preferred_element_type=jnp.float32)
    whole += jnp.dot(parts, table[0, here], preferred_element_type=jnp.float32)
    return fold_rows(whole)


def contract_last(rows, table):
    whole = lax.dot_general(
        in_parts(rows), table, (((1,), (1,)), ((), ())), preferred_element_type=jnp.float32
    )
    whole = fold_rows(whole)
    half = whole.shape[1] // 2
    return whole[:, :half] + whole[:, half:]


def kernel(
    sizes,
    rhs_hbm,
    dual_hbm,
    dirichlet_hbm,
    modes_hbm,
    coarse_hbm,
    partner_hbm,
    sign_hbm,
    count_hbm,
    both,
    modes,
    partner,
    sign_int,
    count,
    stage_dual,
    stage_dirichlet,
    dual,
    dirichlet,
    coarse_own,
    own_table,
    coarse_line,
    coarse_table,
    modes_send,
    modes_own,
    modes_in,
    modes_near,
    given,
    taken_in,
    shared,
    shared_in,
    whole_in,
    near,
    outgoing,
    arriving,
    residual,
    direction,
    mapped,
    image_mapped,
    small,
    sign_ref,
    weight_ref,
    lane_ref,
    tile_ref,
    local_sem,
    rows_send,
    rows_recv,
    take_send,
    take_recv,
    share_send,
    share_recv,
    near_send,
    near_recv,
    modes_sent,
    modes_got,
    whole_sent,
    whole_got,
    halo_send,
    halo_recv,
):
    place = (lax.axis_index("gx"), lax.axis_index("gy"), lax.axis_index("gz"))
    loads, order = rhs_hbm.shape
    x_ref, z_ref = both.at[0], both.at[1]
    modes_total = modes_hbm.shape[0]
    half = sizes[2] // 2
    core = lax.rem(place[2], 2)
    chip = place[2] // 2
    side = place[2] // half
    pack = LANES // modes_total

    def shifted(shifts):
        return tuple(
            lax.rem(place[i] + shifts[i] + sizes[i], sizes[i]) if shifts[i] else place[i]
            for i in range(3)
        )

    def ring(distance, size):
        return min(distance, size - distance)

    takers = sorted(
        ((first, hop) for first in range(sizes[0]) for hop in range(half)),
        key=lambda pair: -ring(pair[0], sizes[0]) - ring(pair[1], half),
    )[:-1]
    sharers = sorted(
        ((second, other) for second in range(sizes[1]) for other in range(2)),
        key=lambda pair: -2 * ring(pair[0], sizes[1]) - pair[1],
    )[:-1]

    def taker(first, hop):
        return (
            lax.rem(place[0] + first, sizes[0]),
            place[1],
            2 * lax.rem(chip + hop, half) + side,
        )

    def sharer(second, other):
        third = 2 * chip + (1 - core) if other else place[2]
        return (place[0], lax.rem(place[1] + second, sizes[1]), third)

    def aside(first, way):
        third = lax.rem(place[2] + way * (2 - 4 * core) + sizes[2], sizes[2])
        return (lax.rem(place[0] + first + sizes[0], sizes[0]), place[1], third)

    sibling = sharer(0, 1)
    keeps = core == side

    loading = [
        pltpu.make_async_copy(rhs_hbm, residual, local_sem.at[0]),
        pltpu.make_async_copy(modes_hbm, modes, local_sem.at[1]),
        pltpu.make_async_copy(sign_hbm, sign_int, local_sem.at[2]),
        pltpu.make_async_copy(partner_hbm, partner, local_sem.at[3]),
        pltpu.make_async_copy(dirichlet_hbm, stage_dirichlet, local_sem.at[4]),
        pltpu.make_async_copy(dual_hbm, stage_dual, local_sem.at[5]),
        pltpu.make_async_copy(count_hbm, count, local_sem.at[7]),
        pltpu.make_async_copy(coarse_hbm, coarse_own, local_sem.at[8]),
    ]
    for number in (0, 1, 2, 3, 6, 7, 4, 5):
        loading[number].start()

    barrier = pltpu.get_barrier_semaphore()
    greeted = 0
    for d in FAR_FIRST:
        pl.semaphore_signal(barrier, inc=1, device_id=shifted(d), device_id_type=MESH)
        greeted += 1
    def greet_giver(first, hop):
        third = half * core + lax.rem(place[2] + hop, half)
        giver = (lax.rem(place[0] + first, sizes[0]), place[1], third)
        pl.semaphore_signal(barrier, inc=1, device_id=giver, device_id_type=MESH)

    for first, hop in takers:
        greet_giver(first, hop)
        greeted += 1

    @pl.when(jnp.logical_not(keeps))
    def _():
        greet_giver(0, 0)

    for first in (-1, 0, 1):
        pl.semaphore_signal(
            barrier, inc=1, device_id=aside(first, -1), device_id_type=MESH
        )
        greeted += 1
    for second, other in sharers:
        pl.semaphore_signal(
            barrier, inc=1, device_id=sharer(second, other), device_id_type=MESH
        )
        greeted += 1

    slot = lax.broadcasted_iota(jnp.int32, (loads, order), 1)
    paired = jnp.zeros((loads, order), jnp.int32)
    for d, start, extent in BLOCKS:
        inside = jnp.int32(1)
        for axis in range(3):
            if d[axis] == -1:
                inside = inside * jnp.where(place[axis] > 0, 1, 0)
            if d[axis] == 1:
                inside = inside * jnp.where(place[axis] < sizes[axis] - 1, 1, 0)
        paired = jnp.where((slot >= start) & (slot < start + extent), inside, paired)
    weight_ref[...] = 1.0 - 0.5 * paired.astype(jnp.float32)
    loading[2].wait()
    sign_ref[...] = jnp.broadcast_to(sign_int[...], (loads, order)).astype(jnp.float32)
    loading[3].wait()
    spread = jnp.broadcast_to(partner[...], (loads, order))
    lane_ref[...] = spread & (LANES - 1)
    tile_ref[...] = jnp.where(paired > 0, spread >> 7, -1)

    loading[1].wait()
    loading[6].wait()
    row = lax.broadcasted_iota(jnp.int32, (modes_total, order), 0)
    used = jnp.where(row < count[0, 0], modes[...], 0.0)
    modes[...] = used
    leading = used.astype(jnp.bfloat16)
    remaining = (used - leading.astype(jnp.float32)).astype(jnp.bfloat16)
    modes_own[0] = leading
    modes_own[1] = remaining
    modes_send[...] = jnp.zeros_like(modes_send)
    spare = lax.rem(place[2] + 1, pack) * modes_total
    quarter = pl.multiple_of(lax.rem(place[2], pack) * modes_total, modes_total)
    modes_send[pl.ds(quarter, modes_total), :] = leading
    modes_send[pl.ds(LANES + quarter, modes_total), :] = remaining

    loading[0].wait()
    pl.semaphore_wait(barrier, greeted + jnp.where(keeps, 0, 1))

    def remote(source, goal, sems, index, peer):
        return pltpu.make_async_remote_copy(
            src_ref=source,
            dst_ref=goal,
            send_sem=sems[0].at[index],
            recv_sem=sems[1].at[index],
            device_id=peer,
            device_id_type=MESH,
        )

    def wait_for(buffer, sems, index):
        copy = remote(buffer, buffer, sems, index, sibling)
        copy.wait_recv()
        copy.wait_send()

    take_sems = (take_send, take_recv)
    share_sems = (share_send, share_recv)

    def gather_start(stage, values, sums):
        message = contract_last(values, modes_send[...]) + in_lanes(sums, spare)
        own = place[0] * half + lax.rem(place[2], half)
        given[stage] = message

        def give(peer):
            remote(given.at[stage], taken_in.at[stage, own], take_sems, stage, peer).start()

        for first, hop in takers:
            give(taker(first, hop))

        @pl.when(keeps)
        def _():
            taken_in[stage, own] = message

        @pl.when(jnp.logical_not(keeps))
        def _():
            give(sibling)

    def collect(stage):
        count = sizes[0] * half

        @pl.when(keeps)
        def _():
            wait_for(taken_in.at[stage, pl.ds(0, count - 1)], take_sems, stage)

        @pl.when(jnp.logical_not(keeps))
        def _():
            wait_for(taken_in.at[stage, pl.ds(0, count)], take_sems, stage)

        pieces = []
        held = [None] * half
        lane = lax.broadcasted_iota(jnp.int32, (loads, LANES), 1)
        sums = jnp.zeros((loads, LANES), jnp.float32)
        for first in range(sizes[0]):
            total = None
            for number in range(half):
                piece = taken_in[stage, first * half + number]
                total = piece if number == 0 else jnp.where(lane < number * modes_total, total, piece)
                held[number] = piece if first == 0 else held[number] + piece
            pieces.append(total)
        for number in range(half):
            start = (number + 1) % pack * modes_total
            inside = (lane >= start) & (lane < start + modes_total)
            sums += jnp.where(inside, held[number], 0.0)
        return jnp.concatenate(pieces, axis=1), sums

    def gather_middle(stage):
        taken, sums = collect(stage)
        partial = contract_last(taken, coarse_table[...])
        message = jnp.concatenate([partial, sums], axis=1)
        shared[stage] = message
        own = core * sizes[1] + place[1]
        shared_in[stage, own] = message
        for second, other in sharers:
            peer = sharer(second, other)
            remote(shared.at[stage], shared_in.at[stage, own], share_sems, stage, peer).start()

    def gather_end(stage):
        count = 2 * sizes[1]
        wait_for(shared_in.at[stage, pl.ds(0, count - 1)], share_sems, stage)
        total = shared_in[stage, 0]
        for number in range(1, count):
            total += shared_in[stage, number]
        sums = total[:, 2 * LANES :]
        sums = sums + pltpu.roll(sums, LANES // 2, 1)
        return total[:, : 2 * LANES], sums + pltpu.roll(sums, LANES // 4, 1)

    near_sems = (near_send, near_recv)

    def near_start(stage, tiles):
        near[stage, :, : 2 * LANES] = tiles
        single = pl.ds(pl.multiple_of((1 - core) * LANES, LANES), LANES)
        for first, at in ((1, 8), (-1, 7), (0, 6)):
            goal = near.at[stage, :, pl.ds(at * LANES, LANES)]
            remote(near.at[stage, :, single], goal, near_sems, stage, aside(first, 1)).start()
        both_tiles = near.at[stage, :, pl.ds(0, 2 * LANES)]
        for first, at in ((1, 4), (-1, 2)):
            goal = near.at[stage, :, pl.ds(at * LANES, 2 * LANES)]
            remote(both_tiles, goal, near_sems, stage, shifted((first, 0, 0))).start()

    def near_end(stage):
        wait_for(near.at[stage, :, pl.ds(2 * LANES, 7 * LANES)], near_sems, stage)
        return near[stage, :, 2 * LANES :]

    def modes_start():
        for d in FAR_FIRST:
            first, last = tiles_of(d)
            at = PLACES[opposite(d)]
            remote(
                modes.at[:, pl.ds(first * LANES, (last - first) * LANES)],
                modes_in.at[:, pl.ds(at * LANES, (last - first) * LANES)],
                (modes_sent, modes_got),
                0,
                shifted(d),
            ).start()

    def modes_end():
        wait_for(modes_in, (modes_sent, modes_got), 0)

        def rows_at(d):
            group = {0: 0, 1: 2, -1: 4}[d[0]]
            outer = {0: 6, 1: 7, -1: 8}[d[0]]
            if d[2] == 0:
                tile = group + core
            elif d[2] == 1:
                tile = jnp.where(core == 0, group + 1, outer)
            else:
                tile = jnp.where(core == 1, group, outer)
            second = lax.rem(place[1] + d[1] + sizes[1], sizes[1])
            return pl.ds(pl.multiple_of(tile * LANES + second * modes_total, modes_total), modes_total)

        def put(rows, lanes, values):
            leading = values.astype(jnp.bfloat16)
            modes_near[0, rows, lanes] = leading
            modes_near[1, rows, lanes] = (values - leading.astype(jnp.float32)).astype(jnp.bfloat16)

        put(rows_at((0, 0, 0)), slice(0, order), modes[...])
        lane = lax.broadcasted_iota(jnp.int32, (modes_total, LANES), 1)
        for d, start, extent in BLOCKS:
            rows = rows_at(d)
            source_first, source_last = tiles_of(opposite(d))
            for tile in range(*tiles_of(d)):
                here = slice(tile * LANES, (tile + 1) * LANES)
                index = jnp.concatenate([lane_ref[:, here]] * (modes_total // loads), axis=0)
                wanted = jnp.concatenate([tile_ref[:, here]] * (modes_total // loads), axis=0)
                slots = lane + tile * LANES
                wanted = jnp.where((slots >= start) & (slots < start + extent), wanted, -1)
                taken = jnp.zeros((modes_total, LANES), jnp.float32)
                for source in range(source_first, source_last):
                    at = (PLACES[d] + source - source_first) * LANES
                    moved = jnp.take_along_axis(
                        modes_in[:, at : at + LANES], index, axis=1, mode="promise_in_bounds"
                    )
                    taken = jnp.where(wanted == source, moved, taken)
                put(rows, here, taken)

    def halo_start(phase, values):
        outgoing[phase] = values
        for d in FAR_FIRST:
            first, last = tiles_of(d)
            at = PLACES[opposite(d)]
            pltpu.make_async_remote_copy(
                src_ref=outgoing.at[phase, :, pl.ds(first * LANES, (last - first) * LANES)],
                dst_ref=arriving.at[phase, :, pl.ds(at * LANES, (last - first) * LANES)],
                send_sem=halo_send.at[phase],
                recv_sem=halo_recv.at[phase],
                device_id=shifted(d),
                device_id_type=MESH,
            ).start()

    def halo_end(phase):
        copy = pltpu.make_async_remote_copy(
            src_ref=arriving.at[phase],
            dst_ref=arriving.at[phase],
            send_sem=halo_send.at[phase],
            recv_sem=halo_recv.at[phase],
            device_id=shifted(BLOCKS[0][0]),
            device_id_type=MESH,
        )
        copy.wait_recv()
        copy.wait_send()
        lane = lax.broadcasted_iota(jnp.int32, (loads, LANES), 1)
        tiles = []
        for tile in range(order // LANES):
            plan = merge_plan(tile)
            merged = None
            for stop, at in reversed(plan):
                piece = arriving[phase, :, at * LANES : (at + 1) * LANES]
                merged = piece if merged is None else jnp.where(lane < stop, piece, merged)
            tiles.append(merged)
        results = []
        for tile in range(order // LANES):
            here = slice(tile * LANES, (tile + 1) * LANES)
            taken = jnp.zeros((loads, LANES), jnp.float32)
            for source in sources_of(tile):
                moved = jnp.take_along_axis(
                    tiles[source], lane_ref[:, here], axis=1, mode="promise_in_bounds"
                )
                taken = jnp.where(tile_ref[:, here] == source, moved, taken)
            results.append(outgoing[phase, :, here] + taken)
        return jnp.concatenate(results, axis=1)

    def local_term(values):
        scaled = weight_ref[...] * sign_ref[...]
        return scaled * product(scaled * values, dirichlet)

    def split_table(source, table):
        step = 64

        def body(i, carry):
            rows = pl.ds(pl.multiple_of(i * step, step), step)
            values = source[rows, :]
            leading = values.astype(jnp.bfloat16)
            table[0, rows, :] = leading
            table[1, rows, :] = (values - leading.astype(jnp.float32)).astype(jnp.bfloat16)
            return carry

        lax.fori_loop(0, order // step, body, 0)

    def inner(former, latter):
        whole = weight_ref[...] * former * latter
        total = whole[:, :LANES]
        for tile in range(1, order // LANES):
            total += whole[:, tile * LANES : (tile + 1) * LANES]
        return jnp.sum(total, axis=1, keepdims=True)

    def in_lanes(columns, start=0):
        lane = lax.broadcasted_iota(jnp.int32, (loads, LANES), 1) - start
        tile = jnp.zeros((loads, LANES), jnp.float32)
        for number, column in enumerate(columns):
            tile = jnp.where(lane == number, column, tile)
        return tile

    gather_start(0, residual[...], [])

    own_place = pl.ds(
        pl.multiple_of(core * LANES + place[1] * modes_total, modes_total), modes_total
    )

    def rows_of(first, second, end):
        start = ((first * sizes[1] + second) * 2 + end) * LANES
        source = coarse_hbm.at[:, pl.ds(pl.multiple_of(start, LANES), LANES)]
        goal = coarse_line.at[own_place, pl.ds(pl.multiple_of(first * LANES, LANES), LANES)]
        return source, goal

    rows_sems = (rows_send, rows_recv)

    def rows_start(begin, end):
        def send_rows(first, carry):
            for second, other in sharers:
                peer = sharer(second, other)
                source, goal = rows_of(first, peer[1], (1 - core) if other else core)
                remote(source, goal, rows_sems, 0, peer).start()
            source, goal = rows_of(first, place[1], core)
            pltpu.make_async_copy(source, goal, local_sem.at[6]).start()
            return carry

        lax.fori_loop(begin, end, send_rows, 0)

    def rows_end():
        rows_total = coarse_line.shape[0]
        wait_for(coarse_line.at[pl.ds(0, rows_total - modes_total), :], rows_sems, 0)
        own = coarse_line.at[pl.ds(0, modes_total), :]
        pltpu.make_async_copy(own, own, local_sem.at[6]).wait()
        rows = coarse_line[...]
        leading = rows.astype(jnp.bfloat16)
        coarse_table[:rows_total, :] = leading
        coarse_table[rows_total:, :] = (rows - leading.astype(jnp.float32)).astype(jnp.bfloat16)

    rows_start(0, sizes[0] // 2)
    modes_near[...] = jnp.zeros_like(modes_near)
    loading[7].wait()
    rows = coarse_own[...]
    leading = rows.astype(jnp.bfloat16)
    own_table[:modes_total, :] = leading
    own_table[modes_total:, :] = (rows - leading.astype(jnp.float32)).astype(jnp.bfloat16)
    loading[4].wait()
    split_table(stage_dirichlet, dirichlet)
    local_now = local_term(residual[...])

    taken, _ = collect(0)
    own = core * sizes[1] + place[1]
    whole_in[own] = taken
    for second, other in sharers:
        peer = sharer(second, other)
        remote(whole_in.at[own], whole_in.at[own], (whole_sent, whole_got), 0, peer).start()
    loading[5].wait()
    split_table(stage_dual, dual)
    zeros = jnp.zeros((loads, order), jnp.float32)
    direction[...] = zeros
    mapped[...] = zeros
    image_mapped[...] = zeros
    x_ref[...] = zeros
    small[...] = jnp.ones((loads, LANES), jnp.float32)
    wait_for(whole_in.at[pl.ds(0, 2 * sizes[1] - 1)], (whole_sent, whole_got), 0)
    pieces = []
    for first in range(sizes[0]):
        for second in range(sizes[1]):
            for end in range(2):
                pieces.append(whole_in[end * sizes[1] + second, :, first * LANES : (first + 1) * LANES])
    coarse = contract_last(jnp.concatenate(pieces, axis=1), own_table[...])
    halo_start(0, local_now + product(coarse, modes_own))
    rows_start(sizes[0] // 2, sizes[0] * 3 // 4)
    z_ref[...] = halo_end(0)

    def step(number, opening):
        stage = number + 1
        image = 2 * number + 1
        sign = sign_ref[...]
        conditioned = z_ref[...]
        halo_start(image, sign * product(sign * conditioned, dual))
        if opening:
            rows_start(sizes[0] * 3 // 4, sizes[0])
        energy_part = inner(residual[...], conditioned)
        cross_part = inner(conditioned, mapped[...])
        fresh = halo_end(image)
        curve_part = inner(conditioned, fresh)
        other_part = inner(direction[...], fresh)
        gather_start(stage, fresh, [energy_part, cross_part, curve_part, other_part])
        halo_start(image + 1, local_term(fresh))
        if opening:
            modes_start()
            rows_end()
        gather_middle(stage)
        if opening:
            modes_end()
        fresh_image = halo_end(image + 1)
        tiles, sums = gather_end(stage)
        near_start(stage, tiles)

        energy = sums[:, 0:1]
        energy_before = small[:, 0:1]
        curve_before = small[:, 1:2]
        beta = jnp.where(number == 0, 0.0, energy / energy_before)
        curve = sums[:, 2:3] + beta * (sums[:, 1:2] + sums[:, 3:4]) + beta * beta * curve_before
        alpha = energy / curve
        small[...] = in_lanes([energy, curve])

        fresh_image = fresh_image + product(tiles, modes_near)
        along_now = conditioned + beta * direction[...]
        direction[...] = along_now
        mapped_now = fresh + beta * mapped[...]
        mapped[...] = mapped_now
        x_ref[...] = x_ref[...] + alpha * along_now
        residual[...] = residual[...] - alpha * mapped_now
        base = fresh_image + beta * image_mapped[...]
        image_now = base + product(near_end(stage), modes_near, 2 * LANES)
        image_mapped[...] = image_now
        z_ref[...] = conditioned - alpha * image_now

    step(0, True)

    def later_step(number, carry):
        step(number, False)
        return carry

    lax.fori_loop(1, DUAL_STEPS, later_step, 0)


def body(
    sizes,
    adjoint_rhs,
    dual_operator,
    dirichlet,
    geneo_modes,
    coarse_inverse,
    partner_slot,
    jump_sign,
    mode_count,
):
    loads, order = adjoint_rhs.shape[3:]
    modes_total, coarse_size = coarse_inverse.shape[3:]
    rows_total = 2 * sizes[1] * modes_total
    columns = coarse_size // (2 * sizes[1])
    stages = DUAL_STEPS + 1
    phases = 2 * DUAL_STEPS + 1
    vector = pltpu.VMEM((loads, order), jnp.float32)
    whole = jax.ShapeDtypeStruct((loads, order), jnp.float32)

    def run(*args):

        return pl.pallas_call(
            functools.partial(kernel, sizes),
            out_shape=jax.ShapeDtypeStruct((2, loads, order), jnp.float32),
            in_specs=[pl.BlockSpec(memory_space=pl.ANY)] * 8,
            out_specs=pl.BlockSpec(memory_space=pltpu.VMEM),
            scratch_shapes=[
                pltpu.VMEM((modes_total, order), jnp.float32),
                pltpu.VMEM((1, order), jnp.int32),
                pltpu.VMEM((1, order), jnp.int32),
                pltpu.SMEM((1, 1), jnp.int32),
                pltpu.VMEM((order, order), jnp.float32),
                pltpu.VMEM((order, order), jnp.float32),
                pltpu.VMEM((2, order, order), jnp.bfloat16),
                pltpu.VMEM((2, order, order), jnp.bfloat16),
                pltpu.VMEM((modes_total, coarse_size), jnp.float32),
                pltpu.VMEM((2 * modes_total, coarse_size), jnp.bfloat16),
                pltpu.VMEM((rows_total, columns), jnp.float32),
                pltpu.VMEM((2 * rows_total, columns), jnp.bfloat16),
                pltpu.VMEM((2 * LANES, order), jnp.bfloat16),
                pltpu.VMEM((2, modes_total, order), jnp.bfloat16),
                pltpu.VMEM((modes_total, ARRIVING * LANES), jnp.float32),
                pltpu.VMEM((2, 9 * LANES, order), jnp.bfloat16),
                pltpu.VMEM((stages, loads, LANES), jnp.float32),
                pltpu.VMEM((stages, sizes[0] * sizes[2] // 2, loads, LANES), jnp.float32),
                pltpu.VMEM((stages, loads, 3 * LANES), jnp.float32),
                pltpu.VMEM((stages, 2 * sizes[1], loads, 3 * LANES), jnp.float32),
                pltpu.VMEM((2 * sizes[1], loads, columns), jnp.float32),
                pltpu.VMEM((stages, loads, 9 * LANES), jnp.float32),
                pltpu.VMEM((phases, loads, order), jnp.float32),
                pltpu.VMEM((phases, loads, ARRIVING * LANES), jnp.float32),
                vector,
                vector,
                vector,
                vector,
                pltpu.VMEM((loads, LANES), jnp.float32),
                vector,
                vector,
                pltpu.VMEM((loads, order), jnp.int32),
                pltpu.VMEM((loads, order), jnp.int32),
                pltpu.SemaphoreType.DMA((9,)),
                pltpu.SemaphoreType.DMA((1,)),
                pltpu.SemaphoreType.DMA((1,)),
                pltpu.SemaphoreType.DMA((stages,)),
                pltpu.SemaphoreType.DMA((stages,)),
                pltpu.SemaphoreType.DMA((stages,)),
                pltpu.SemaphoreType.DMA((stages,)),
                pltpu.SemaphoreType.DMA((stages,)),
                pltpu.SemaphoreType.DMA((stages,)),
                pltpu.SemaphoreType.DMA((1,)),
                pltpu.SemaphoreType.DMA((1,)),
                pltpu.SemaphoreType.DMA((1,)),
                pltpu.SemaphoreType.DMA((1,)),
                pltpu.SemaphoreType.DMA((phases,)),
                pltpu.SemaphoreType.DMA((phases,)),
            ],
            compiler_params=pltpu.CompilerParams(
                collective_id=0, has_side_effects=True, vmem_limit_bytes=56 * 1024 * 1024
            ),
        )(*args)

    both = run(
        adjoint_rhs.reshape(loads, order),
        dual_operator.reshape(order, order),
        dirichlet.reshape(order, order),
        geneo_modes.reshape(modes_total, order),
        coarse_inverse.reshape(modes_total, coarse_size),
        partner_slot.reshape(1, order),
        jump_sign.reshape(1, order),
        mode_count.reshape(1, 1),
    )
    found, force = both[0], both[1]
    return found.reshape(adjoint_rhs.shape), force.reshape(adjoint_rhs.shape)


def solution(mesh):

    sizes = (mesh.shape["gx"], mesh.shape["gy"], mesh.shape["gz"])
    spot = ("gx", "gy", "gz")
    placed = (
        P(*spot, None, None),
        P(*spot, None, None),
        P(*spot, None, None),
        P(*spot, None, None),
        P(*spot, None, None),
        P(*spot, None),
        P(*spot, None),
        P(*spot),
    )
    return jax.shard_map(
        functools.partial(body, sizes),
        mesh=mesh,
        in_specs=placed,
        out_specs=(P(*spot, None, None), P(*spot, None, None)),
        check_vma=False,
    )
```

```python
import functools

import jax
import jax.numpy as jnp
from jax import lax
from jax.experimental import pallas as pl
from jax.experimental.pallas import tpu as pltpu
from jax.sharding import PartitionSpec as P

FACE_SLOTS = 144
EDGE_SLOTS = 12
CORNER_SLOTS = 2
DUAL_STEPS = 3
LANES = 128
MESH = pl.DeviceIdType.MESH


def block_list():
    blocks = []
    cursor = 0
    for first in (-1, 0, 1):
        for second in (-1, 0, 1):
            for third in (-1, 0, 1):
                nonzero = abs(first) + abs(second) + abs(third)
                if nonzero == 0:
                    continue
                extent = (FACE_SLOTS, EDGE_SLOTS, CORNER_SLOTS)[nonzero - 1]
                blocks.append(((first, second, third), cursor, extent))
                cursor += extent
    return blocks


BLOCKS = block_list()
FAR_FIRST = sorted((record[0] for record in BLOCKS), key=lambda d: -sum(map(abs, d)))
SPAN = {d: (start, start + extent) for d, start, extent in BLOCKS}


def opposite(d):
    return (-d[0], -d[1], -d[2])


def tiles_of(d):
    start, stop = SPAN[d]
    return start // LANES, (stop - 1) // LANES + 1


def arrival_places():
    places = {}
    cursor = 0
    for d, _, _ in BLOCKS:
        first, last = tiles_of(opposite(d))
        places[d] = cursor
        cursor += last - first
    return places, cursor


PLACES, ARRIVING = arrival_places()


def merge_plan(tile):
    plan = []
    for d, _, _ in sorted(BLOCKS, key=lambda record: SPAN[opposite(record[0])]):
        source = opposite(d)
        first, last = tiles_of(source)
        if first <= tile < last:
            plan.append((min(SPAN[source][1] - tile * LANES, LANES), PLACES[d] + tile - first))
    return plan


def sources_of(tile):
    found = set()
    for d, _, _ in BLOCKS:
        first, last = tiles_of(d)
        if first <= tile < last:
            found.update(range(*tiles_of(opposite(d))))
    return sorted(found)


def in_parts(values):
    leading = values.astype(jnp.bfloat16).astype(jnp.float32)
    return jnp.concatenate([values, values - leading], axis=0).astype(jnp.bfloat16)


def fold_rows(values):
    rows = values.shape[0] // 2
    return values[:rows] + values[rows:]


def product(rows, table, start=0):
    parts = in_parts(rows)
    here = slice(start, start + rows.shape[1])
    whole = jnp.dot(parts, table[1, here], preferred_element_type=jnp.float32)
    whole += jnp.dot(parts, table[0, here], preferred_element_type=jnp.float32)
    return fold_rows(whole)


def contract_last(rows, table):
    whole = lax.dot_general(
        in_parts(rows), table, (((1,), (1,)), ((), ())), preferred_element_type=jnp.float32
    )
    whole = fold_rows(whole)
    half = whole.shape[1] // 2
    return whole[:, :half] + whole[:, half:]


def kernel(
    sizes,
    rhs_hbm,
    dual_hbm,
    dirichlet_hbm,
    modes_hbm,
    coarse_hbm,
    partner_hbm,
    sign_hbm,
    count_hbm,
    both,
    modes,
    partner,
    sign_int,
    count,
    stage_dual,
    stage_dirichlet,
    dual,
    dirichlet,
    coarse_own,
    own_table,
    coarse_line,
    coarse_table,
    modes_send,
    modes_own,
    modes_in,
    modes_near,
    given,
    taken_in,
    shared,
    shared_in,
    whole_in,
    near,
    outgoing,
    arriving,
    residual,
    direction,
    mapped,
    image_mapped,
    small,
    sign_ref,
    weight_ref,
    lane_ref,
    tile_ref,
    local_sem,
    rows_send,
    rows_recv,
    take_send,
    take_recv,
    share_send,
    share_recv,
    near_send,
    near_recv,
    modes_sent,
    modes_got,
    whole_sent,
    whole_got,
    halo_send,
    halo_recv,
):
    place = (lax.axis_index("gx"), lax.axis_index("gy"), lax.axis_index("gz"))
    loads, order = rhs_hbm.shape
    x_ref, z_ref = both.at[0], both.at[1]
    modes_total = modes_hbm.shape[0]
    half = sizes[2] // 2
    core = lax.rem(place[2], 2)
    chip = place[2] // 2
    side = place[2] // half
    pack = LANES // modes_total

    def shifted(shifts):
        return tuple(
            lax.rem(place[i] + shifts[i] + sizes[i], sizes[i]) if shifts[i] else place[i]
            for i in range(3)
        )

    def ring(distance, size):
        return min(distance, size - distance)

    takers = sorted(
        ((first, hop) for first in range(sizes[0]) for hop in range(half)),
        key=lambda pair: -ring(pair[0], sizes[0]) - ring(pair[1], half),
    )[:-1]
    sharers = sorted(
        ((second, other) for second in range(sizes[1]) for other in range(2)),
        key=lambda pair: -2 * ring(pair[0], sizes[1]) - pair[1],
    )[:-1]

    def taker(first, hop):
        return (
            lax.rem(place[0] + first, sizes[0]),
            place[1],
            2 * lax.rem(chip + hop, half) + side,
        )

    def sharer(second, other):
        third = 2 * chip + (1 - core) if other else place[2]
        return (place[0], lax.rem(place[1] + second, sizes[1]), third)

    def aside(first, way):
        third = lax.rem(place[2] + way * (2 - 4 * core) + sizes[2], sizes[2])
        return (lax.rem(place[0] + first + sizes[0], sizes[0]), place[1], third)

    sibling = sharer(0, 1)
    keeps = core == side

    loading = [
        pltpu.make_async_copy(rhs_hbm, residual, local_sem.at[0]),
        pltpu.make_async_copy(modes_hbm, modes, local_sem.at[1]),
        pltpu.make_async_copy(sign_hbm, sign_int, local_sem.at[2]),
        pltpu.make_async_copy(partner_hbm, partner, local_sem.at[3]),
        pltpu.make_async_copy(dirichlet_hbm, stage_dirichlet, local_sem.at[4]),
        pltpu.make_async_copy(dual_hbm, stage_dual, local_sem.at[5]),
        pltpu.make_async_copy(count_hbm, count, local_sem.at[7]),
        pltpu.make_async_copy(coarse_hbm, coarse_own, local_sem.at[8]),
    ]
    for number in (0, 1, 2, 3, 6, 7, 4, 5):
        loading[number].start()

    barrier = pltpu.get_barrier_semaphore()
    greeted = 0
    def greet_giver(first, hop):
        third = half * core + lax.rem(place[2] + hop, half)
        giver = (lax.rem(place[0] + first, sizes[0]), place[1], third)
        pl.semaphore_signal(barrier, inc=1, device_id=giver, device_id_type=MESH)

    for first, hop in takers:
        greet_giver(first, hop)
        greeted += 1

    @pl.when(jnp.logical_not(keeps))
    def _():
        greet_giver(0, 0)

    for second, other in sharers:
        pl.semaphore_signal(
            barrier, inc=1, device_id=sharer(second, other), device_id_type=MESH
        )
        greeted += 1

    slot = lax.broadcasted_iota(jnp.int32, (loads, order), 1)
    paired = jnp.zeros((loads, order), jnp.int32)
    for d, start, extent in BLOCKS:
        inside = jnp.int32(1)
        for axis in range(3):
            if d[axis] == -1:
                inside = inside * jnp.where(place[axis] > 0, 1, 0)
            if d[axis] == 1:
                inside = inside * jnp.where(place[axis] < sizes[axis] - 1, 1, 0)
        paired = jnp.where((slot >= start) & (slot < start + extent), inside, paired)
    weight_ref[...] = 1.0 - 0.5 * paired.astype(jnp.float32)
    loading[2].wait()
    sign_ref[...] = jnp.broadcast_to(sign_int[...], (loads, order)).astype(jnp.float32)
    loading[3].wait()
    spread = jnp.broadcast_to(partner[...], (loads, order))
    lane_ref[...] = spread & (LANES - 1)
    tile_ref[...] = jnp.where(paired > 0, spread >> 7, -1)

    loading[1].wait()
    loading[6].wait()
    row = lax.broadcasted_iota(jnp.int32, (modes_total, order), 0)
    used = jnp.where(row < count[0, 0], modes[...], 0.0)
    modes[...] = used
    leading = used.astype(jnp.bfloat16)
    remaining = (used - leading.astype(jnp.float32)).astype(jnp.bfloat16)
    modes_own[0] = leading
    modes_own[1] = remaining
    modes_send[...] = jnp.zeros_like(modes_send)
    spare = lax.rem(place[2] + 1, pack) * modes_total
    quarter = pl.multiple_of(lax.rem(place[2], pack) * modes_total, modes_total)
    modes_send[pl.ds(quarter, modes_total), :] = leading
    modes_send[pl.ds(LANES + quarter, modes_total), :] = remaining

    loading[0].wait()

    def remote(source, goal, sems, index, peer):
        return pltpu.make_async_remote_copy(
            src_ref=source,
            dst_ref=goal,
            send_sem=sems[0].at[index],
            recv_sem=sems[1].at[index],
            device_id=peer,
            device_id_type=MESH,
        )

    def wait_for(buffer, sems, index):
        copy = remote(buffer, buffer, sems, index, sibling)
        copy.wait_recv()
        copy.wait_send()

    take_sems = (take_send, take_recv)
    share_sems = (share_send, share_recv)

    def gather_start(stage, values, sums, before=None):
        message = contract_last(values, modes_send[...]) + in_lanes(sums, spare)
        own = place[0] * half + lax.rem(place[2], half)
        given[stage] = message
        if before is not None:
            before()

        def give(peer):
            remote(given.at[stage], taken_in.at[stage, own], take_sems, stage, peer).start()

        for first, hop in takers:
            give(taker(first, hop))

        @pl.when(keeps)
        def _():
            taken_in[stage, own] = message

        @pl.when(jnp.logical_not(keeps))
        def _():
            give(sibling)

    def collect(stage):
        count = sizes[0] * half

        @pl.when(keeps)
        def _():
            wait_for(taken_in.at[stage, pl.ds(0, count - 1)], take_sems, stage)

        @pl.when(jnp.logical_not(keeps))
        def _():
            wait_for(taken_in.at[stage, pl.ds(0, count)], take_sems, stage)

        pieces = []
        held = [None] * half
        lane = lax.broadcasted_iota(jnp.int32, (loads, LANES), 1)
        sums = jnp.zeros((loads, LANES), jnp.float32)
        for first in range(sizes[0]):
            total = None
            for number in range(half):
                piece = taken_in[stage, first * half + number]
                total = piece if number == 0 else jnp.where(lane < number * modes_total, total, piece)
                held[number] = piece if first == 0 else held[number] + piece
            pieces.append(total)
        for number in range(half):
            start = (number + 1) % pack * modes_total
            inside = (lane >= start) & (lane < start + modes_total)
            sums += jnp.where(inside, held[number], 0.0)
        return jnp.concatenate(pieces, axis=1), sums

    def gather_middle(stage):
        taken, sums = collect(stage)
        partial = contract_last(taken, coarse_table[...])
        message = jnp.concatenate([partial, sums], axis=1)
        shared[stage] = message
        own = core * sizes[1] + place[1]
        shared_in[stage, own] = message
        for second, other in sharers:
            peer = sharer(second, other)
            remote(shared.at[stage], shared_in.at[stage, own], share_sems, stage, peer).start()

    def gather_end(stage):
        count = 2 * sizes[1]
        wait_for(shared_in.at[stage, pl.ds(0, count - 1)], share_sems, stage)
        total = shared_in[stage, 0]
        for number in range(1, count):
            total += shared_in[stage, number]
        sums = total[:, 2 * LANES :]
        sums = sums + pltpu.roll(sums, LANES // 2, 1)
        return total[:, : 2 * LANES], sums + pltpu.roll(sums, LANES // 4, 1)

    near_sems = (near_send, near_recv)

    def near_start(stage, tiles):
        near[stage, :, : 2 * LANES] = tiles
        single = pl.ds(pl.multiple_of((1 - core) * LANES, LANES), LANES)
        for first, at in ((1, 8), (-1, 7), (0, 6)):
            goal = near.at[stage, :, pl.ds(at * LANES, LANES)]
            remote(near.at[stage, :, single], goal, near_sems, stage, aside(first, 1)).start()
        both_tiles = near.at[stage, :, pl.ds(0, 2 * LANES)]
        for first, at in ((1, 4), (-1, 2)):
            goal = near.at[stage, :, pl.ds(at * LANES, 2 * LANES)]
            remote(both_tiles, goal, near_sems, stage, shifted((first, 0, 0))).start()

    def near_end(stage):
        wait_for(near.at[stage, :, pl.ds(2 * LANES, 7 * LANES)], near_sems, stage)
        return near[stage, :, 2 * LANES :]

    def modes_start():
        for d in FAR_FIRST:
            first, last = tiles_of(d)
            at = PLACES[opposite(d)]
            remote(
                modes.at[:, pl.ds(first * LANES, (last - first) * LANES)],
                modes_in.at[:, pl.ds(at * LANES, (last - first) * LANES)],
                (modes_sent, modes_got),
                0,
                shifted(d),
            ).start()

    def modes_end():
        wait_for(modes_in, (modes_sent, modes_got), 0)

        def rows_at(d):
            group = {0: 0, 1: 2, -1: 4}[d[0]]
            outer = {0: 6, 1: 7, -1: 8}[d[0]]
            if d[2] == 0:
                tile = group + core
            elif d[2] == 1:
                tile = jnp.where(core == 0, group + 1, outer)
            else:
                tile = jnp.where(core == 1, group, outer)
            second = lax.rem(place[1] + d[1] + sizes[1], sizes[1])
            return pl.ds(pl.multiple_of(tile * LANES + second * modes_total, modes_total), modes_total)

        def put(rows, lanes, values):
            leading = values.astype(jnp.bfloat16)
            modes_near[0, rows, lanes] = leading
            modes_near[1, rows, lanes] = (values - leading.astype(jnp.float32)).astype(jnp.bfloat16)

        put(rows_at((0, 0, 0)), slice(0, order), modes[...])
        lane = lax.broadcasted_iota(jnp.int32, (modes_total, LANES), 1)
        for d, start, extent in BLOCKS:
            rows = rows_at(d)
            source_first, source_last = tiles_of(opposite(d))
            for tile in range(*tiles_of(d)):
                here = slice(tile * LANES, (tile + 1) * LANES)
                index = jnp.concatenate([lane_ref[:, here]] * (modes_total // loads), axis=0)
                wanted = jnp.concatenate([tile_ref[:, here]] * (modes_total // loads), axis=0)
                slots = lane + tile * LANES
                wanted = jnp.where((slots >= start) & (slots < start + extent), wanted, -1)
                taken = jnp.zeros((modes_total, LANES), jnp.float32)
                for source in range(source_first, source_last):
                    at = (PLACES[d] + source - source_first) * LANES
                    moved = jnp.take_along_axis(
                        modes_in[:, at : at + LANES], index, axis=1, mode="promise_in_bounds"
                    )
                    taken = jnp.where(wanted == source, moved, taken)
                put(rows, here, taken)

    def halo_start(phase, values, begin=0):
        outgoing[phase, :, begin : begin + values.shape[1]] = values
        for d in FAR_FIRST:
            if SPAN[d][0] < begin or SPAN[d][1] > begin + values.shape[1]:
                continue
            first, last = tiles_of(d)
            at = PLACES[opposite(d)]
            pltpu.make_async_remote_copy(
                src_ref=outgoing.at[phase, :, pl.ds(first * LANES, (last - first) * LANES)],
                dst_ref=arriving.at[phase, :, pl.ds(at * LANES, (last - first) * LANES)],
                send_sem=halo_send.at[phase],
                recv_sem=halo_recv.at[phase],
                device_id=shifted(d),
                device_id_type=MESH,
            ).start()

    def halo_end(phase):
        copy = pltpu.make_async_remote_copy(
            src_ref=arriving.at[phase],
            dst_ref=arriving.at[phase],
            send_sem=halo_send.at[phase],
            recv_sem=halo_recv.at[phase],
            device_id=shifted(BLOCKS[0][0]),
            device_id_type=MESH,
        )
        copy.wait_recv()
        copy.wait_send()
        lane = lax.broadcasted_iota(jnp.int32, (loads, LANES), 1)
        tiles = []
        for tile in range(order // LANES):
            plan = merge_plan(tile)
            merged = None
            for stop, at in reversed(plan):
                piece = arriving[phase, :, at * LANES : (at + 1) * LANES]
                merged = piece if merged is None else jnp.where(lane < stop, piece, merged)
            tiles.append(merged)
        results = []
        for tile in range(order // LANES):
            here = slice(tile * LANES, (tile + 1) * LANES)
            taken = jnp.zeros((loads, LANES), jnp.float32)
            for source in sources_of(tile):
                moved = jnp.take_along_axis(
                    tiles[source], lane_ref[:, here], axis=1, mode="promise_in_bounds"
                )
                taken = jnp.where(tile_ref[:, here] == source, moved, taken)
            results.append(outgoing[phase, :, here] + taken)
        return jnp.concatenate(results, axis=1)

    def local_term(values):
        scaled = weight_ref[...] * sign_ref[...]
        return scaled * product(scaled * values, dirichlet)

    def split_table(source, table):
        step = 64

        def body(i, carry):
            rows = pl.ds(pl.multiple_of(i * step, step), step)
            values = source[rows, :]
            leading = values.astype(jnp.bfloat16)
            table[0, rows, :] = leading
            table[1, rows, :] = (values - leading.astype(jnp.float32)).astype(jnp.bfloat16)
            return carry

        lax.fori_loop(0, order // step, body, 0)

    def inner(former, latter):
        whole = weight_ref[...] * former * latter
        total = whole[:, :LANES]
        for tile in range(1, order // LANES):
            total += whole[:, tile * LANES : (tile + 1) * LANES]
        return jnp.sum(total, axis=1, keepdims=True)

    def in_lanes(columns, start=0):
        lane = lax.broadcasted_iota(jnp.int32, (loads, LANES), 1) - start
        tile = jnp.zeros((loads, LANES), jnp.float32)
        for number, column in enumerate(columns):
            tile = jnp.where(lane == number, column, tile)
        return tile

    def all_here():
        pl.semaphore_wait(barrier, greeted + jnp.where(keeps, 0, 1))

    gather_start(0, residual[...], [], all_here)

    own_place = pl.ds(
        pl.multiple_of(core * LANES + place[1] * modes_total, modes_total), modes_total
    )

    def rows_of(first, second, end):
        start = ((first * sizes[1] + second) * 2 + end) * LANES
        source = coarse_hbm.at[:, pl.ds(pl.multiple_of(start, LANES), LANES)]
        goal = coarse_line.at[own_place, pl.ds(pl.multiple_of(first * LANES, LANES), LANES)]
        return source, goal

    rows_sems = (rows_send, rows_recv)

    def rows_start(begin, end):
        def send_rows(first, carry):
            for second, other in sharers:
                peer = sharer(second, other)
                source, goal = rows_of(first, peer[1], (1 - core) if other else core)
                remote(source, goal, rows_sems, 0, peer).start()
            source, goal = rows_of(first, place[1], core)
            pltpu.make_async_copy(source, goal, local_sem.at[6]).start()
            return carry

        lax.fori_loop(begin, end, send_rows, 0)

    def rows_end():
        rows_total = coarse_line.shape[0]
        wait_for(coarse_line.at[pl.ds(0, rows_total - modes_total), :], rows_sems, 0)
        own = coarse_line.at[pl.ds(0, modes_total), :]
        pltpu.make_async_copy(own, own, local_sem.at[6]).wait()
        rows = coarse_line[...]
        leading = rows.astype(jnp.bfloat16)
        coarse_table[:rows_total, :] = leading
        coarse_table[rows_total:, :] = (rows - leading.astype(jnp.float32)).astype(jnp.bfloat16)

    rows_start(0, sizes[0] // 2)
    modes_near[...] = jnp.zeros_like(modes_near)
    loading[7].wait()
    rows = coarse_own[...]
    leading = rows.astype(jnp.bfloat16)
    own_table[:modes_total, :] = leading
    own_table[modes_total:, :] = (rows - leading.astype(jnp.float32)).astype(jnp.bfloat16)
    loading[4].wait()
    split_table(stage_dirichlet, dirichlet)
    local_now = local_term(residual[...])

    taken, _ = collect(0)
    own = core * sizes[1] + place[1]
    whole_in[own] = taken
    for second, other in sharers:
        peer = sharer(second, other)
        remote(whole_in.at[own], whole_in.at[own], (whole_sent, whole_got), 0, peer).start()
    loading[5].wait()
    split_table(stage_dual, dual)
    zeros = jnp.zeros((loads, order), jnp.float32)
    direction[...] = zeros
    mapped[...] = zeros
    image_mapped[...] = zeros
    x_ref[...] = zeros
    small[...] = jnp.ones((loads, LANES), jnp.float32)
    wait_for(whole_in.at[pl.ds(0, 2 * sizes[1] - 1)], (whole_sent, whole_got), 0)
    pieces = []
    for first in range(sizes[0]):
        for second in range(sizes[1]):
            for end in range(2):
                pieces.append(whole_in[end * sizes[1] + second, :, first * LANES : (first + 1) * LANES])
    coarse = contract_last(jnp.concatenate(pieces, axis=1), own_table[...])
    halo_start(0, local_now + product(coarse, modes_own))
    rows_start(sizes[0] // 2, sizes[0] * 3 // 4)
    z_ref[...] = halo_end(0)

    def step(number, opening):
        stage = number + 1
        image = 2 * number + 1
        sign = sign_ref[...]
        conditioned = z_ref[...]
        parts = in_parts(sign * conditioned)
        for begin in (0, order // 2):
            columns = slice(begin, begin + order // 2)
            mapped_part = jnp.dot(parts, dual[1, :, columns], preferred_element_type=jnp.float32)
            mapped_part += jnp.dot(parts, dual[0, :, columns], preferred_element_type=jnp.float32)
            halo_start(image, sign[:, columns] * fold_rows(mapped_part), begin)
        if opening:
            rows_start(sizes[0] * 3 // 4, sizes[0])
        energy_part = inner(residual[...], conditioned)
        cross_part = inner(conditioned, mapped[...])
        fresh = halo_end(image)
        curve_part = inner(conditioned, fresh)
        other_part = inner(direction[...], fresh)
        gather_start(stage, fresh, [energy_part, cross_part, curve_part, other_part])
        halo_start(image + 1, local_term(fresh))
        if opening:
            modes_start()
            rows_end()
        gather_middle(stage)
        if opening:
            modes_end()
        fresh_image = halo_end(image + 1)
        tiles, sums = gather_end(stage)
        near_start(stage, tiles)

        energy = sums[:, 0:1]
        energy_before = small[:, 0:1]
        curve_before = small[:, 1:2]
        beta = jnp.where(number == 0, 0.0, energy / energy_before)
        curve = sums[:, 2:3] + beta * (sums[:, 1:2] + sums[:, 3:4]) + beta * beta * curve_before
        alpha = energy / curve
        small[...] = in_lanes([energy, curve])

        fresh_image = fresh_image + product(tiles, modes_near)
        along_now = conditioned + beta * direction[...]
        direction[...] = along_now
        mapped_now = fresh + beta * mapped[...]
        mapped[...] = mapped_now
        x_ref[...] = x_ref[...] + alpha * along_now
        residual[...] = residual[...] - alpha * mapped_now
        base = fresh_image + beta * image_mapped[...]
        image_now = base + product(near_end(stage), modes_near, 2 * LANES)
        image_mapped[...] = image_now
        z_ref[...] = conditioned - alpha * image_now

    step(0, True)

    def later_step(number, carry):
        step(number, False)
        return carry

    lax.fori_loop(1, DUAL_STEPS, later_step, 0)


def body(
    sizes,
    adjoint_rhs,
    dual_operator,
    dirichlet,
    geneo_modes,
    coarse_inverse,
    partner_slot,
    jump_sign,
    mode_count,
):
    loads, order = adjoint_rhs.shape[3:]
    modes_total, coarse_size = coarse_inverse.shape[3:]
    rows_total = 2 * sizes[1] * modes_total
    columns = coarse_size // (2 * sizes[1])
    stages = DUAL_STEPS + 1
    phases = 2 * DUAL_STEPS + 1
    vector = pltpu.VMEM((loads, order), jnp.float32)
    whole = jax.ShapeDtypeStruct((loads, order), jnp.float32)

    def run(*args):

        return pl.pallas_call(
            functools.partial(kernel, sizes),
            out_shape=jax.ShapeDtypeStruct((2, loads, order), jnp.float32),
            in_specs=[pl.BlockSpec(memory_space=pl.ANY)] * 8,
            out_specs=pl.BlockSpec(memory_space=pltpu.VMEM),
            scratch_shapes=[
                pltpu.VMEM((modes_total, order), jnp.float32),
                pltpu.VMEM((1, order), jnp.int32),
                pltpu.VMEM((1, order), jnp.int32),
                pltpu.SMEM((1, 1), jnp.int32),
                pltpu.VMEM((order, order), jnp.float32),
                pltpu.VMEM((order, order), jnp.float32),
                pltpu.VMEM((2, order, order), jnp.bfloat16),
                pltpu.VMEM((2, order, order), jnp.bfloat16),
                pltpu.VMEM((modes_total, coarse_size), jnp.float32),
                pltpu.VMEM((2 * modes_total, coarse_size), jnp.bfloat16),
                pltpu.VMEM((rows_total, columns), jnp.float32),
                pltpu.VMEM((2 * rows_total, columns), jnp.bfloat16),
                pltpu.VMEM((2 * LANES, order), jnp.bfloat16),
                pltpu.VMEM((2, modes_total, order), jnp.bfloat16),
                pltpu.VMEM((modes_total, ARRIVING * LANES), jnp.float32),
                pltpu.VMEM((2, 9 * LANES, order), jnp.bfloat16),
                pltpu.VMEM((stages, loads, LANES), jnp.float32),
                pltpu.VMEM((stages, sizes[0] * sizes[2] // 2, loads, LANES), jnp.float32),
                pltpu.VMEM((stages, loads, 3 * LANES), jnp.float32),
                pltpu.VMEM((stages, 2 * sizes[1], loads, 3 * LANES), jnp.float32),
                pltpu.VMEM((2 * sizes[1], loads, columns), jnp.float32),
                pltpu.VMEM((stages, loads, 9 * LANES), jnp.float32),
                pltpu.VMEM((phases, loads, order), jnp.float32),
                pltpu.VMEM((phases, loads, ARRIVING * LANES), jnp.float32),
                vector,
                vector,
                vector,
                vector,
                pltpu.VMEM((loads, LANES), jnp.float32),
                vector,
                vector,
                pltpu.VMEM((loads, order), jnp.int32),
                pltpu.VMEM((loads, order), jnp.int32),
                pltpu.SemaphoreType.DMA((9,)),
                pltpu.SemaphoreType.DMA((1,)),
                pltpu.SemaphoreType.DMA((1,)),
                pltpu.SemaphoreType.DMA((stages,)),
                pltpu.SemaphoreType.DMA((stages,)),
                pltpu.SemaphoreType.DMA((stages,)),
                pltpu.SemaphoreType.DMA((stages,)),
                pltpu.SemaphoreType.DMA((stages,)),
                pltpu.SemaphoreType.DMA((stages,)),
                pltpu.SemaphoreType.DMA((1,)),
                pltpu.SemaphoreType.DMA((1,)),
                pltpu.SemaphoreType.DMA((1,)),
                pltpu.SemaphoreType.DMA((1,)),
                pltpu.SemaphoreType.DMA((phases,)),
                pltpu.SemaphoreType.DMA((phases,)),
            ],
            compiler_params=pltpu.CompilerParams(
                collective_id=0, has_side_effects=True, vmem_limit_bytes=56 * 1024 * 1024
            ),
        )(*args)

    both = run(
        adjoint_rhs.reshape(loads, order),
        dual_operator.reshape(order, order),
        dirichlet.reshape(order, order),
        geneo_modes.reshape(modes_total, order),
        coarse_inverse.reshape(modes_total, coarse_size),
        partner_slot.reshape(1, order),
        jump_sign.reshape(1, order),
        mode_count.reshape(1, 1),
    )
    found, force = both[0], both[1]
    return found.reshape(adjoint_rhs.shape), force.reshape(adjoint_rhs.shape)


def solution(mesh):

    sizes = (mesh.shape["gx"], mesh.shape["gy"], mesh.shape["gz"])
    spot = ("gx", "gy", "gz")
    placed = (
        P(*spot, None, None),
        P(*spot, None, None),
        P(*spot, None, None),
        P(*spot, None, None),
        P(*spot, None, None),
        P(*spot, None),
        P(*spot, None),
        P(*spot),
    )
    return jax.shard_map(
        functools.partial(body, sizes),
        mesh=mesh,
        in_specs=placed,
        out_specs=(P(*spot, None, None), P(*spot, None, None)),
        check_vma=False,
    )
```

```python
import functools

import jax
import jax.numpy as jnp
from jax import lax
from jax.experimental import pallas as pl
from jax.experimental.pallas import tpu as pltpu
from jax.sharding import PartitionSpec as P

FACE_SLOTS = 144
EDGE_SLOTS = 12
CORNER_SLOTS = 2
DUAL_STEPS = 3
LANES = 128
MESH = pl.DeviceIdType.MESH


def block_list():
    blocks = []
    cursor = 0
    for first in (-1, 0, 1):
        for second in (-1, 0, 1):
            for third in (-1, 0, 1):
                nonzero = abs(first) + abs(second) + abs(third)
                if nonzero == 0:
                    continue
                extent = (FACE_SLOTS, EDGE_SLOTS, CORNER_SLOTS)[nonzero - 1]
                blocks.append(((first, second, third), cursor, extent))
                cursor += extent
    return blocks


BLOCKS = block_list()
FAR_FIRST = sorted((record[0] for record in BLOCKS), key=lambda d: -sum(map(abs, d)))
SPAN = {d: (start, start + extent) for d, start, extent in BLOCKS}


def opposite(d):
    return (-d[0], -d[1], -d[2])


def tiles_of(d):
    start, stop = SPAN[d]
    return start // LANES, (stop - 1) // LANES + 1


def arrival_places():
    places = {}
    cursor = 0
    for d, _, _ in BLOCKS:
        first, last = tiles_of(opposite(d))
        places[d] = cursor
        cursor += last - first
    return places, cursor


PLACES, ARRIVING = arrival_places()


def merge_plan(tile):
    plan = []
    for d, _, _ in sorted(BLOCKS, key=lambda record: SPAN[opposite(record[0])]):
        source = opposite(d)
        first, last = tiles_of(source)
        if first <= tile < last:
            plan.append((min(SPAN[source][1] - tile * LANES, LANES), PLACES[d] + tile - first))
    return plan


def sources_of(tile):
    found = set()
    for d, _, _ in BLOCKS:
        first, last = tiles_of(d)
        if first <= tile < last:
            found.update(range(*tiles_of(opposite(d))))
    return sorted(found)


def in_parts(values):
    leading = values.astype(jnp.bfloat16).astype(jnp.float32)
    return jnp.concatenate([values, values - leading], axis=0).astype(jnp.bfloat16)


def fold_rows(values):
    rows = values.shape[0] // 2
    return values[:rows] + values[rows:]


def product(rows, table, start=0):
    parts = in_parts(rows)
    here = slice(start, start + rows.shape[1])
    whole = jnp.dot(parts, table[1, here], preferred_element_type=jnp.float32)
    whole += jnp.dot(parts, table[0, here], preferred_element_type=jnp.float32)
    return fold_rows(whole)


def contract_last(rows, table):
    whole = lax.dot_general(
        in_parts(rows), table, (((1,), (1,)), ((), ())), preferred_element_type=jnp.float32
    )
    whole = fold_rows(whole)
    half = whole.shape[1] // 2
    return whole[:, :half] + whole[:, half:]


def kernel(
    sizes,
    rhs_hbm,
    dual_hbm,
    dirichlet_hbm,
    modes_hbm,
    coarse_hbm,
    partner_hbm,
    sign_hbm,
    count_hbm,
    both,
    modes,
    partner,
    sign_int,
    count,
    stage_dual,
    stage_dirichlet,
    dual,
    dirichlet,
    coarse_own,
    own_table,
    coarse_line,
    coarse_table,
    modes_send,
    modes_own,
    modes_in,
    modes_near,
    given,
    taken_in,
    shared,
    shared_in,
    whole_in,
    near,
    outgoing,
    arriving,
    residual,
    direction,
    mapped,
    image_mapped,
    small,
    sign_ref,
    weight_ref,
    lane_ref,
    tile_ref,
    local_sem,
    rows_send,
    rows_recv,
    take_send,
    take_recv,
    share_send,
    share_recv,
    near_send,
    near_recv,
    modes_sent,
    modes_got,
    whole_sent,
    whole_got,
    halo_send,
    halo_recv,
):
    place = (lax.axis_index("gx"), lax.axis_index("gy"), lax.axis_index("gz"))
    loads, order = rhs_hbm.shape
    x_ref, z_ref = both.at[0], both.at[1]
    modes_total = modes_hbm.shape[0]
    half = sizes[2] // 2
    core = lax.rem(place[2], 2)
    chip = place[2] // 2
    side = place[2] // half
    pack = LANES // modes_total

    def shifted(shifts):
        return tuple(
            lax.rem(place[i] + shifts[i] + sizes[i], sizes[i]) if shifts[i] else place[i]
            for i in range(3)
        )

    def ring(distance, size):
        return min(distance, size - distance)

    takers = sorted(
        ((first, hop) for first in range(sizes[0]) for hop in range(half)),
        key=lambda pair: -ring(pair[0], sizes[0]) - ring(pair[1], half),
    )[:-1]
    sharers = sorted(
        ((second, other) for second in range(sizes[1]) for other in range(2)),
        key=lambda pair: -2 * ring(pair[0], sizes[1]) - pair[1],
    )[:-1]

    def taker(first, hop):
        return (
            lax.rem(place[0] + first, sizes[0]),
            place[1],
            2 * lax.rem(chip + hop, half) + side,
        )

    def sharer(second, other):
        third = 2 * chip + (1 - core) if other else place[2]
        return (place[0], lax.rem(place[1] + second, sizes[1]), third)

    def aside(first, way):
        third = lax.rem(place[2] + way * (2 - 4 * core) + sizes[2], sizes[2])
        return (lax.rem(place[0] + first + sizes[0], sizes[0]), place[1], third)

    sibling = sharer(0, 1)
    keeps = core == side

    loading = [
        pltpu.make_async_copy(rhs_hbm, residual, local_sem.at[0]),
        pltpu.make_async_copy(modes_hbm, modes, local_sem.at[1]),
        pltpu.make_async_copy(sign_hbm, sign_int, local_sem.at[2]),
        pltpu.make_async_copy(partner_hbm, partner, local_sem.at[3]),
        pltpu.make_async_copy(dirichlet_hbm, stage_dirichlet, local_sem.at[4]),
        pltpu.make_async_copy(dual_hbm, stage_dual, local_sem.at[5]),
        pltpu.make_async_copy(count_hbm, count, local_sem.at[7]),
        pltpu.make_async_copy(coarse_hbm, coarse_own, local_sem.at[8]),
    ]
    for number in (0, 1, 2, 3, 6, 7, 4, 5):
        loading[number].start()

    barrier = pltpu.get_barrier_semaphore()
    greeted = 0
    def greet_giver(first, hop):
        third = half * core + lax.rem(place[2] + hop, half)
        giver = (lax.rem(place[0] + first, sizes[0]), place[1], third)
        pl.semaphore_signal(barrier, inc=1, device_id=giver, device_id_type=MESH)

    for first, hop in takers:
        greet_giver(first, hop)
        greeted += 1

    @pl.when(jnp.logical_not(keeps))
    def _():
        greet_giver(0, 0)

    for second, other in sharers:
        pl.semaphore_signal(
            barrier, inc=1, device_id=sharer(second, other), device_id_type=MESH
        )
        greeted += 1

    loading[1].wait()
    loading[6].wait()
    row = lax.broadcasted_iota(jnp.int32, (modes_total, order), 0)
    used = jnp.where(row < count[0, 0], modes[...], 0.0)
    modes[...] = used
    leading = used.astype(jnp.bfloat16)
    remaining = (used - leading.astype(jnp.float32)).astype(jnp.bfloat16)
    modes_own[0] = leading
    modes_own[1] = remaining
    modes_send[...] = jnp.zeros_like(modes_send)
    spare = lax.rem(place[2] + 1, pack) * modes_total
    quarter = pl.multiple_of(lax.rem(place[2], pack) * modes_total, modes_total)
    modes_send[pl.ds(quarter, modes_total), :] = leading
    modes_send[pl.ds(LANES + quarter, modes_total), :] = remaining

    loading[0].wait()

    def remote(source, goal, sems, index, peer):
        return pltpu.make_async_remote_copy(
            src_ref=source,
            dst_ref=goal,
            send_sem=sems[0].at[index],
            recv_sem=sems[1].at[index],
            device_id=peer,
            device_id_type=MESH,
        )

    def wait_for(buffer, sems, index):
        copy = remote(buffer, buffer, sems, index, sibling)
        copy.wait_recv()
        copy.wait_send()

    take_sems = (take_send, take_recv)
    share_sems = (share_send, share_recv)

    def gather_start(stage, values, sums, before=None):
        message = contract_last(values, modes_send[...]) + in_lanes(sums, spare)
        own = place[0] * half + lax.rem(place[2], half)
        given[stage] = message
        if before is not None:
            before()

        def give(peer):
            remote(given.at[stage], taken_in.at[stage, own], take_sems, stage, peer).start()

        for first, hop in takers:
            give(taker(first, hop))

        @pl.when(keeps)
        def _():
            taken_in[stage, own] = message

        @pl.when(jnp.logical_not(keeps))
        def _():
            give(sibling)

    def collect(stage):
        count = sizes[0] * half

        @pl.when(keeps)
        def _():
            wait_for(taken_in.at[stage, pl.ds(0, count - 1)], take_sems, stage)

        @pl.when(jnp.logical_not(keeps))
        def _():
            wait_for(taken_in.at[stage, pl.ds(0, count)], take_sems, stage)

        pieces = []
        held = [None] * half
        lane = lax.broadcasted_iota(jnp.int32, (loads, LANES), 1)
        sums = jnp.zeros((loads, LANES), jnp.float32)
        for first in range(sizes[0]):
            total = None
            for number in range(half):
                piece = taken_in[stage, first * half + number]
                total = piece if number == 0 else jnp.where(lane < number * modes_total, total, piece)
                held[number] = piece if first == 0 else held[number] + piece
            pieces.append(total)
        for number in range(half):
            start = (number + 1) % pack * modes_total
            inside = (lane >= start) & (lane < start + modes_total)
            sums += jnp.where(inside, held[number], 0.0)
        return jnp.concatenate(pieces, axis=1), sums

    def gather_middle(stage):
        taken, sums = collect(stage)
        partial = contract_last(taken, coarse_table[...])
        message = jnp.concatenate([partial, sums], axis=1)
        shared[stage] = message
        own = core * sizes[1] + place[1]
        shared_in[stage, own] = message
        for second, other in sharers:
            peer = sharer(second, other)
            remote(shared.at[stage], shared_in.at[stage, own], share_sems, stage, peer).start()

    def gather_end(stage):
        count = 2 * sizes[1]
        wait_for(shared_in.at[stage, pl.ds(0, count - 1)], share_sems, stage)
        total = shared_in[stage, 0]
        for number in range(1, count):
            total += shared_in[stage, number]
        sums = total[:, 2 * LANES :]
        sums = sums + pltpu.roll(sums, LANES // 2, 1)
        return total[:, : 2 * LANES], sums + pltpu.roll(sums, LANES // 4, 1)

    near_sems = (near_send, near_recv)

    def near_start(stage, tiles):
        near[stage, :, : 2 * LANES] = tiles
        single = pl.ds(pl.multiple_of((1 - core) * LANES, LANES), LANES)
        for first, at in ((1, 8), (-1, 7), (0, 6)):
            goal = near.at[stage, :, pl.ds(at * LANES, LANES)]
            remote(near.at[stage, :, single], goal, near_sems, stage, aside(first, 1)).start()
        both_tiles = near.at[stage, :, pl.ds(0, 2 * LANES)]
        for first, at in ((1, 4), (-1, 2)):
            goal = near.at[stage, :, pl.ds(at * LANES, 2 * LANES)]
            remote(both_tiles, goal, near_sems, stage, shifted((first, 0, 0))).start()

    def near_end(stage):
        wait_for(near.at[stage, :, pl.ds(2 * LANES, 7 * LANES)], near_sems, stage)
        return near[stage, :, 2 * LANES :]

    def modes_start():
        for d in FAR_FIRST:
            first, last = tiles_of(d)
            at = PLACES[opposite(d)]
            remote(
                modes.at[:, pl.ds(first * LANES, (last - first) * LANES)],
                modes_in.at[:, pl.ds(at * LANES, (last - first) * LANES)],
                (modes_sent, modes_got),
                0,
                shifted(d),
            ).start()

    def modes_end():
        wait_for(modes_in, (modes_sent, modes_got), 0)

        def rows_at(d):
            group = {0: 0, 1: 2, -1: 4}[d[0]]
            outer = {0: 6, 1: 7, -1: 8}[d[0]]
            if d[2] == 0:
                tile = group + core
            elif d[2] == 1:
                tile = jnp.where(core == 0, group + 1, outer)
            else:
                tile = jnp.where(core == 1, group, outer)
            second = lax.rem(place[1] + d[1] + sizes[1], sizes[1])
            return pl.ds(pl.multiple_of(tile * LANES + second * modes_total, modes_total), modes_total)

        def put(rows, lanes, values):
            leading = values.astype(jnp.bfloat16)
            modes_near[0, rows, lanes] = leading
            modes_near[1, rows, lanes] = (values - leading.astype(jnp.float32)).astype(jnp.bfloat16)

        put(rows_at((0, 0, 0)), slice(0, order), modes[...])
        lane = lax.broadcasted_iota(jnp.int32, (modes_total, LANES), 1)
        for d, start, extent in BLOCKS:
            rows = rows_at(d)
            source_first, source_last = tiles_of(opposite(d))
            for tile in range(*tiles_of(d)):
                here = slice(tile * LANES, (tile + 1) * LANES)
                index = jnp.concatenate([lane_ref[:, here]] * (modes_total // loads), axis=0)
                wanted = jnp.concatenate([tile_ref[:, here]] * (modes_total // loads), axis=0)
                slots = lane + tile * LANES
                wanted = jnp.where((slots >= start) & (slots < start + extent), wanted, -1)
                taken = jnp.zeros((modes_total, LANES), jnp.float32)
                for source in range(source_first, source_last):
                    at = (PLACES[d] + source - source_first) * LANES
                    moved = jnp.take_along_axis(
                        modes_in[:, at : at + LANES], index, axis=1, mode="promise_in_bounds"
                    )
                    taken = jnp.where(wanted == source, moved, taken)
                put(rows, here, taken)

    def halo_start(phase, values):
        outgoing[phase] = values
        for d in FAR_FIRST:
            first, last = tiles_of(d)
            at = PLACES[opposite(d)]
            pltpu.make_async_remote_copy(
                src_ref=outgoing.at[phase, :, pl.ds(first * LANES, (last - first) * LANES)],
                dst_ref=arriving.at[phase, :, pl.ds(at * LANES, (last - first) * LANES)],
                send_sem=halo_send.at[phase],
                recv_sem=halo_recv.at[phase],
                device_id=shifted(d),
                device_id_type=MESH,
            ).start()

    def halo_end(phase):
        copy = pltpu.make_async_remote_copy(
            src_ref=arriving.at[phase],
            dst_ref=arriving.at[phase],
            send_sem=halo_send.at[phase],
            recv_sem=halo_recv.at[phase],
            device_id=shifted(BLOCKS[0][0]),
            device_id_type=MESH,
        )
        copy.wait_recv()
        copy.wait_send()
        lane = lax.broadcasted_iota(jnp.int32, (loads, LANES), 1)
        tiles = []
        for tile in range(order // LANES):
            plan = merge_plan(tile)
            merged = None
            for stop, at in reversed(plan):
                piece = arriving[phase, :, at * LANES : (at + 1) * LANES]
                merged = piece if merged is None else jnp.where(lane < stop, piece, merged)
            tiles.append(merged)
        results = []
        for tile in range(order // LANES):
            here = slice(tile * LANES, (tile + 1) * LANES)
            taken = jnp.zeros((loads, LANES), jnp.float32)
            for source in sources_of(tile):
                moved = jnp.take_along_axis(
                    tiles[source], lane_ref[:, here], axis=1, mode="promise_in_bounds"
                )
                taken = jnp.where(tile_ref[:, here] == source, moved, taken)
            results.append(outgoing[phase, :, here] + taken)
        return jnp.concatenate(results, axis=1)

    def local_term(values):
        scaled = weight_ref[...] * sign_ref[...]
        return scaled * product(scaled * values, dirichlet)

    def split_table(source, table):
        step = 64

        def body(i, carry):
            rows = pl.ds(pl.multiple_of(i * step, step), step)
            values = source[rows, :]
            leading = values.astype(jnp.bfloat16)
            table[0, rows, :] = leading
            table[1, rows, :] = (values - leading.astype(jnp.float32)).astype(jnp.bfloat16)
            return carry

        lax.fori_loop(0, order // step, body, 0)

    def inner(former, latter):
        whole = weight_ref[...] * former * latter
        total = whole[:, :LANES]
        for tile in range(1, order // LANES):
            total += whole[:, tile * LANES : (tile + 1) * LANES]
        return jnp.sum(total, axis=1, keepdims=True)

    def in_lanes(columns, start=0):
        lane = lax.broadcasted_iota(jnp.int32, (loads, LANES), 1) - start
        tile = jnp.zeros((loads, LANES), jnp.float32)
        for number, column in enumerate(columns):
            tile = jnp.where(lane == number, column, tile)
        return tile

    def all_here():
        pl.semaphore_wait(barrier, greeted + jnp.where(keeps, 0, 1))

    gather_start(0, residual[...], [], all_here)

    slot = lax.broadcasted_iota(jnp.int32, (loads, order), 1)
    paired = jnp.zeros((loads, order), jnp.int32)
    for d, start, extent in BLOCKS:
        inside = jnp.int32(1)
        for axis in range(3):
            if d[axis] == -1:
                inside = inside * jnp.where(place[axis] > 0, 1, 0)
            if d[axis] == 1:
                inside = inside * jnp.where(place[axis] < sizes[axis] - 1, 1, 0)
        paired = jnp.where((slot >= start) & (slot < start + extent), inside, paired)
    weight_ref[...] = 1.0 - 0.5 * paired.astype(jnp.float32)
    loading[2].wait()
    sign_ref[...] = jnp.broadcast_to(sign_int[...], (loads, order)).astype(jnp.float32)
    loading[3].wait()
    spread = jnp.broadcast_to(partner[...], (loads, order))
    lane_ref[...] = spread & (LANES - 1)
    tile_ref[...] = jnp.where(paired > 0, spread >> 7, -1)

    own_place = pl.ds(
        pl.multiple_of(core * LANES + place[1] * modes_total, modes_total), modes_total
    )

    def rows_of(first, second, end):
        start = ((first * sizes[1] + second) * 2 + end) * LANES
        source = coarse_hbm.at[:, pl.ds(pl.multiple_of(start, LANES), LANES)]
        goal = coarse_line.at[own_place, pl.ds(pl.multiple_of(first * LANES, LANES), LANES)]
        return source, goal

    rows_sems = (rows_send, rows_recv)

    def rows_start(begin, end):
        def send_rows(first, carry):
            for second, other in sharers:
                peer = sharer(second, other)
                source, goal = rows_of(first, peer[1], (1 - core) if other else core)
                remote(source, goal, rows_sems, 0, peer).start()
            source, goal = rows_of(first, place[1], core)
            pltpu.make_async_copy(source, goal, local_sem.at[6]).start()
            return carry

        lax.fori_loop(begin, end, send_rows, 0)

    def rows_end():
        rows_total = coarse_line.shape[0]
        wait_for(coarse_line.at[pl.ds(0, rows_total - modes_total), :], rows_sems, 0)
        own = coarse_line.at[pl.ds(0, modes_total), :]
        pltpu.make_async_copy(own, own, local_sem.at[6]).wait()
        rows = coarse_line[...]
        leading = rows.astype(jnp.bfloat16)
        coarse_table[:rows_total, :] = leading
        coarse_table[rows_total:, :] = (rows - leading.astype(jnp.float32)).astype(jnp.bfloat16)

    rows_start(0, 2)
    modes_near[...] = jnp.zeros_like(modes_near)
    loading[7].wait()
    rows = coarse_own[...]
    leading = rows.astype(jnp.bfloat16)
    own_table[:modes_total, :] = leading
    own_table[modes_total:, :] = (rows - leading.astype(jnp.float32)).astype(jnp.bfloat16)
    loading[4].wait()
    split_table(stage_dirichlet, dirichlet)
    local_now = local_term(residual[...])

    taken, _ = collect(0)
    own = core * sizes[1] + place[1]
    whole_in[own] = taken
    for second, other in sharers:
        peer = sharer(second, other)
        remote(whole_in.at[own], whole_in.at[own], (whole_sent, whole_got), 0, peer).start()
    loading[5].wait()
    split_table(stage_dual, dual)
    zeros = jnp.zeros((loads, order), jnp.float32)
    direction[...] = zeros
    mapped[...] = zeros
    image_mapped[...] = zeros
    x_ref[...] = zeros
    small[...] = jnp.ones((loads, LANES), jnp.float32)
    wait_for(whole_in.at[pl.ds(0, 2 * sizes[1] - 1)], (whole_sent, whole_got), 0)
    pieces = []
    for first in range(sizes[0]):
        for second in range(sizes[1]):
            for end in range(2):
                pieces.append(whole_in[end * sizes[1] + second, :, first * LANES : (first + 1) * LANES])
    coarse = contract_last(jnp.concatenate(pieces, axis=1), own_table[...])
    halo_start(0, local_now + product(coarse, modes_own))
    rows_start(2, 5)
    z_ref[...] = halo_end(0)

    def step(number, opening):
        stage = number + 1
        image = 2 * number + 1
        sign = sign_ref[...]
        conditioned = z_ref[...]
        halo_start(image, sign * product(sign * conditioned, dual))
        if opening:
            rows_start(5, sizes[0])
        energy_part = inner(residual[...], conditioned)
        cross_part = inner(conditioned, mapped[...])
        fresh = halo_end(image)
        curve_part = inner(conditioned, fresh)
        other_part = inner(direction[...], fresh)
        gather_start(stage, fresh, [energy_part, cross_part, curve_part, other_part])
        halo_start(image + 1, local_term(fresh))
        if opening:
            modes_start()
            rows_end()
        gather_middle(stage)
        if opening:
            modes_end()
        fresh_image = halo_end(image + 1)
        tiles, sums = gather_end(stage)
        near_start(stage, tiles)

        energy = sums[:, 0:1]
        energy_before = small[:, 0:1]
        curve_before = small[:, 1:2]
        beta = jnp.where(number == 0, 0.0, energy / energy_before)
        curve = sums[:, 2:3] + beta * (sums[:, 1:2] + sums[:, 3:4]) + beta * beta * curve_before
        alpha = energy / curve
        small[...] = in_lanes([energy, curve])

        fresh_image = fresh_image + product(tiles, modes_near)
        along_now = conditioned + beta * direction[...]
        direction[...] = along_now
        mapped_now = fresh + beta * mapped[...]
        mapped[...] = mapped_now
        x_ref[...] = x_ref[...] + alpha * along_now
        residual[...] = residual[...] - alpha * mapped_now
        base = fresh_image + beta * image_mapped[...]
        image_now = base + product(near_end(stage), modes_near, 2 * LANES)
        image_mapped[...] = image_now
        z_ref[...] = conditioned - alpha * image_now

    step(0, True)

    def later_step(number, carry):
        step(number, False)
        return carry

    lax.fori_loop(1, DUAL_STEPS, later_step, 0)


def body(
    sizes,
    adjoint_rhs,
    dual_operator,
    dirichlet,
    geneo_modes,
    coarse_inverse,
    partner_slot,
    jump_sign,
    mode_count,
):
    loads, order = adjoint_rhs.shape[3:]
    modes_total, coarse_size = coarse_inverse.shape[3:]
    rows_total = 2 * sizes[1] * modes_total
    columns = coarse_size // (2 * sizes[1])
    stages = DUAL_STEPS + 1
    phases = 2 * DUAL_STEPS + 1
    vector = pltpu.VMEM((loads, order), jnp.float32)
    whole = jax.ShapeDtypeStruct((loads, order), jnp.float32)

    def run(*args):

        return pl.pallas_call(
            functools.partial(kernel, sizes),
            out_shape=jax.ShapeDtypeStruct((2, loads, order), jnp.float32),
            in_specs=[pl.BlockSpec(memory_space=pl.ANY)] * 8,
            out_specs=pl.BlockSpec(memory_space=pltpu.VMEM),
            scratch_shapes=[
                pltpu.VMEM((modes_total, order), jnp.float32),
                pltpu.VMEM((1, order), jnp.int32),
                pltpu.VMEM((1, order), jnp.int32),
                pltpu.SMEM((1, 1), jnp.int32),
                pltpu.VMEM((order, order), jnp.float32),
                pltpu.VMEM((order, order), jnp.float32),
                pltpu.VMEM((2, order, order), jnp.bfloat16),
                pltpu.VMEM((2, order, order), jnp.bfloat16),
                pltpu.VMEM((modes_total, coarse_size), jnp.float32),
                pltpu.VMEM((2 * modes_total, coarse_size), jnp.bfloat16),
                pltpu.VMEM((rows_total, columns), jnp.float32),
                pltpu.VMEM((2 * rows_total, columns), jnp.bfloat16),
                pltpu.VMEM((2 * LANES, order), jnp.bfloat16),
                pltpu.VMEM((2, modes_total, order), jnp.bfloat16),
                pltpu.VMEM((modes_total, ARRIVING * LANES), jnp.float32),
                pltpu.VMEM((2, 9 * LANES, order), jnp.bfloat16),
                pltpu.VMEM((stages, loads, LANES), jnp.float32),
                pltpu.VMEM((stages, sizes[0] * sizes[2] // 2, loads, LANES), jnp.float32),
                pltpu.VMEM((stages, loads, 3 * LANES), jnp.float32),
                pltpu.VMEM((stages, 2 * sizes[1], loads, 3 * LANES), jnp.float32),
                pltpu.VMEM((2 * sizes[1], loads, columns), jnp.float32),
                pltpu.VMEM((stages, loads, 9 * LANES), jnp.float32),
                pltpu.VMEM((phases, loads, order), jnp.float32),
                pltpu.VMEM((phases, loads, ARRIVING * LANES), jnp.float32),
                vector,
                vector,
                vector,
                vector,
                pltpu.VMEM((loads, LANES), jnp.float32),
                vector,
                vector,
                pltpu.VMEM((loads, order), jnp.int32),
                pltpu.VMEM((loads, order), jnp.int32),
                pltpu.SemaphoreType.DMA((9,)),
                pltpu.SemaphoreType.DMA((1,)),
                pltpu.SemaphoreType.DMA((1,)),
                pltpu.SemaphoreType.DMA((stages,)),
                pltpu.SemaphoreType.DMA((stages,)),
                pltpu.SemaphoreType.DMA((stages,)),
                pltpu.SemaphoreType.DMA((stages,)),
                pltpu.SemaphoreType.DMA((stages,)),
                pltpu.SemaphoreType.DMA((stages,)),
                pltpu.SemaphoreType.DMA((1,)),
                pltpu.SemaphoreType.DMA((1,)),
                pltpu.SemaphoreType.DMA((1,)),
                pltpu.SemaphoreType.DMA((1,)),
                pltpu.SemaphoreType.DMA((phases,)),
                pltpu.SemaphoreType.DMA((phases,)),
            ],
            compiler_params=pltpu.CompilerParams(
                collective_id=0, has_side_effects=True, vmem_limit_bytes=56 * 1024 * 1024
            ),
        )(*args)

    both = run(
        adjoint_rhs.reshape(loads, order),
        dual_operator.reshape(order, order),
        dirichlet.reshape(order, order),
        geneo_modes.reshape(modes_total, order),
        coarse_inverse.reshape(modes_total, coarse_size),
        partner_slot.reshape(1, order),
        jump_sign.reshape(1, order),
        mode_count.reshape(1, 1),
    )
    found, force = both[0], both[1]
    return found.reshape(adjoint_rhs.shape), force.reshape(adjoint_rhs.shape)


def solution(mesh):

    sizes = (mesh.shape["gx"], mesh.shape["gy"], mesh.shape["gz"])
    spot = ("gx", "gy", "gz")
    placed = (
        P(*spot, None, None),
        P(*spot, None, None),
        P(*spot, None, None),
        P(*spot, None, None),
        P(*spot, None, None),
        P(*spot, None),
        P(*spot, None),
        P(*spot),
    )
    return jax.shard_map(
        functools.partial(body, sizes),
        mesh=mesh,
        in_specs=placed,
        out_specs=(P(*spot, None, None), P(*spot, None, None)),
        check_vma=False,
    )
```
